128 devices in a mesh: grp: 16 (over z, x), lane: 8 (over y, core).
Axes of the slice: x: 4, y: 4, z: 4, core: 2. Of those that a mesh axis runs over, the one named last changes fastest.
Arguments:
- coords: float32 [3, 786432], P(None, ('grp', 'lane')), may hold values from 0 to 1, as said below
- charges: float32 [64, 786432], P(None, ('grp', 'lane')), may hold values from -0.9 to 0.9
- basis: float32 [256, 196608], P(None, ('grp', 'lane')), may hold values from -0.75 to 0.75
- transfer1: float32 [64, 196608], P(None, ('grp', 'lane')), may hold values from -0.375 to 0.375
- transfer2: float32 [64, 49152], P(None, ('grp', 'lane')), may hold values from -0.75 to 0.75
- coupling0: float32 [8, 64, 196608], P(None, None, ('grp', 'lane')), may hold values from -0.25 to 0.25
- coupling1: float32 [4, 64, 49152], P(None, None, ('grp', 'lane')), may hold values from -0.375 to 0.375
- coupling2: float32 [4, 64, 1024], P(None, None, 'grp'), may hold values from -0.375 to 0.375
- near_list: int32 [3072, 9], P(('grp', 'lane')), may hold values from 0 to 3071, as said below
- near_count: int32 [3072], P(('grp', 'lane')), may hold values from 2 to 9
- far0_list: int32 [3072, 8], P(('grp', 'lane')), may hold values from 0 to 3071, as said below
- far1_list: int32 [768, 4], P(('grp', 'lane')), may hold values from 0 to 767, as said below
- far2_list: int32 [16, 4], replicated, may hold values from 0 to 15, as said below
Outputs:
- potential: float32 [64, 786432], P(None, ('grp', 'lane'))
The draws below stay inside these ranges and needn't reach their ends.
Inputs may be any that keep to these rules, and one draw needn't show every extreme that they name: `coords`: the points lie on a torus inside the unit cube; the points of one leaf form a small patch of it, and leaves close in order are close on the surface. `near_list`: row l starts with l itself; its other entries are distinct leaves 1 to 24 positions away from l, cyclically over 3072, and none of them stands in row l of far0_list. `far0_list`: distinct leaves 1 to 24 positions away from l, cyclically over 3072. `far1_list`: distinct middle clusters 1 to 6 positions away from m, cyclically over 768. `far2_list`: distinct top clusters other than g.
All inputs are finite; a program needn't handle non-finite values.
Results may differ from the reference program's by a relative error of at most 0.0003.
Values sent between devices are 32-bit elements; how exact they have to be, the bound alone decides.
A program may use at most 128 MiB of HBM per device.

```python
import math
import jax
import jax.numpy as jnp
from jax import lax

P_SIZE = 256
R = 64
NRHS = 64
LEAF_DEV = 24
CHILD = 4
NEAR = 9
FAR0 = 8
FAR1 = 4
FAR2 = 4
MID_DEV = 6
LEAVES = 3072
POINTS = 786432
MIDS = 768
TOPS = 16
MIDS_TOP = 48


def leaf_offsets(key):
    scores = jax.random.randint(key, (LEAVES, 2 * LEAF_DEV), 0, 1 << 20) * (2 * LEAF_DEV) + jnp.arange(2 * LEAF_DEV, dtype=jnp.int32)
    ranking = jnp.argsort(scores, axis=1, stable=True)
    places = jnp.arange(2 * LEAF_DEV, dtype=jnp.int32)
    shifts = jnp.where(places < LEAF_DEV, places - LEAF_DEV, places - LEAF_DEV + 1)
    return shifts[ranking]


def draw_coords(key, part):
    key = jax.random.fold_in(key, 6)
    key_u, key_v = jax.random.split(key)
    tile_leaves = 1
    level_bits = 0
    while LEAVES % (tile_leaves * 4) == 0:
        tile_leaves = tile_leaves * 4
        level_bits = level_bits + 1
    side = 1 << level_bits
    strips = LEAVES // tile_leaves
    leaf = jnp.arange(POINTS, dtype=jnp.int32) // P_SIZE
    inner = leaf % tile_leaves
    strip = leaf // tile_leaves
    cell_u = jnp.zeros_like(leaf)
    cell_v = jnp.zeros_like(leaf)
    for level in range(level_bits):
        cell_u = cell_u + (inner >> 2 * level & 1) * (1 << level)
        cell_v = cell_v + (inner >> 2 * level + 1 & 1) * (1 << level)
    jitter_u = jax.random.uniform(key_u, (POINTS,), jnp.float32)
    jitter_v = jax.random.uniform(key_v, (POINTS,), jnp.float32)
    angle_u = 2.0 * math.pi * ((cell_u + strip * side).astype(jnp.float32) + jitter_u) / float(side * strips)
    angle_v = 2.0 * math.pi * (cell_v.astype(jnp.float32) + jitter_v) / float(side)
    radius = 0.3 + 0.15 * jnp.cos(angle_v)
    first = 0.5 + radius * jnp.cos(angle_u)
    second = 0.5 + radius * jnp.sin(angle_u)
    third = 0.5 + 0.15 * jnp.sin(angle_v)
    return jnp.stack([first, second, third], axis=0).astype(jnp.float32)


def draw_near_list(key, part):
    shifts = leaf_offsets(key)
    chosen = jnp.concatenate([jnp.zeros((LEAVES, 1), jnp.int32), shifts[:, :NEAR - 1]], axis=1)
    return ((jnp.arange(LEAVES, dtype=jnp.int32)[:, None] + chosen) % LEAVES).astype(jnp.int32)


def draw_far0_list(key, part):
    shifts = leaf_offsets(key)
    chosen = shifts[:, NEAR - 1:NEAR - 1 + FAR0]
    return ((jnp.arange(LEAVES, dtype=jnp.int32)[:, None] + chosen) % LEAVES).astype(jnp.int32)


def draw_near_count(key, part):
    key = jax.random.fold_in(key, 3)
    key_heavy, key_light = jax.random.split(key)
    owners = LEAVES // LEAF_DEV
    heavy = jax.random.randint(key_heavy, (owners,), 0, 4) == 0
    heavy = jnp.where(jnp.arange(owners) == 0, True, heavy)
    light = jax.random.randint(key_light, (LEAVES,), 2, 6)
    return jnp.where(jnp.repeat(heavy, LEAF_DEV), NEAR, light).astype(jnp.int32)


def draw_far1_list(key, part):
    key = jax.random.fold_in(key, 4)
    scores = jax.random.randint(key, (MIDS, 2 * MID_DEV), 0, 1 << 20) * (2 * MID_DEV) + jnp.arange(2 * MID_DEV, dtype=jnp.int32)
    ranking = jnp.argsort(scores, axis=1, stable=True)
    places = jnp.arange(2 * MID_DEV, dtype=jnp.int32)
    shifts = jnp.where(places < MID_DEV, places - MID_DEV, places - MID_DEV + 1)[ranking][:, :FAR1]
    return ((jnp.arange(MIDS, dtype=jnp.int32)[:, None] + shifts) % MIDS).astype(jnp.int32)


def draw_far2_list(key, part):
    key = jax.random.fold_in(key, 5)
    scores = jax.random.randint(key, (TOPS, TOPS), 0, 1 << 20) * TOPS + jnp.arange(TOPS, dtype=jnp.int32)
    scores = jnp.where(jnp.eye(TOPS, dtype=bool), 1 << 30, scores)
    ranking = jnp.argsort(scores, axis=1, stable=True)
    return ranking[:, :FAR2].astype(jnp.int32)


def level_of(rng, extent, cuts, smallest, high):
    gain = 1.0
    for dim, parts in cuts:
        draws = jax.random.uniform(jax.random.fold_in(jax.random.fold_in(rng, 6), dim), (parts,), jnp.float32, smallest / len(cuts), high / len(cuts))
        gain = gain * jnp.repeat(jnp.exp(draws), extent[dim] // parts).reshape((-1,) + (1,) * (len(extent) - 1 - dim))
    return gain


def centred(key, extent, deviation, most, cuts=(), held_as=jnp.bfloat16):
    level = level_of(key, extent, cuts, -0.22, 0.18) if cuts else 1.0
    array = jax.random.normal(key, extent, jnp.float32) * deviation * level
    return jnp.minimum(jnp.maximum(array, -most), most).astype(held_as)


def setup_inputs(seed: int = 0) -> dict:
    keys = jax.random.split(jax.random.key(seed), 14)
    return {
        "coords": draw_coords(jax.random.fold_in(keys[13], 71), 0),
        "charges": centred(keys[1], (NRHS, POINTS), 0.15, 0.9, ((1, 128),), jnp.float32),
        "basis": centred(keys[2], (P_SIZE, LEAVES * R), R ** -0.5, 0.75, ((1, 128),), jnp.float32),
        "transfer1": centred(keys[3], (R, LEAVES * R), (R * CHILD) ** -0.5, 0.375, ((1, 128),), jnp.float32),
        "transfer2": centred(keys[4], (R, MIDS * R), R ** -0.5, 0.75, ((1, 128),), jnp.float32),
        "coupling0": centred(keys[5], (FAR0, R, LEAVES * R), (R * FAR0) ** -0.5, 0.25, ((2, 128),), jnp.float32),
        "coupling1": centred(keys[6], (FAR1, R, MIDS * R), (R * FAR1) ** -0.5, 0.375, ((2, 128),), jnp.float32),
        "coupling2": centred(keys[7], (FAR2, R, TOPS * R), (R * FAR2) ** -0.5, 0.375, ((2, 16),), jnp.float32),
        "near_list": draw_near_list(jax.random.fold_in(keys[13], 71), 0),
        "near_count": draw_near_count(jax.random.fold_in(keys[13], 71), 0),
        "far0_list": draw_far0_list(jax.random.fold_in(keys[13], 71), 0),
        "far1_list": draw_far1_list(jax.random.fold_in(keys[13], 71), 0),
        "far2_list": draw_far2_list(jax.random.fold_in(keys[13], 71), 0),
    }


inv_four_pi = 1.0 / (4.0 * math.pi)
smooth_sq = 5e-05
highest = lax.Precision.HIGHEST

def kernel_block(targets, sources):
    dist_sq = jnp.zeros((targets.shape[1], sources.shape[1]), jnp.float32)
    for comp in range(3):
        diffs = targets[comp][:, None] - sources[comp][None, :]
        dist_sq = dist_sq + diffs * diffs
    return inv_four_pi / jnp.sqrt(dist_sq + smooth_sq)

def reference(coords, charges, basis, transfer1, transfer2, coupling0, coupling1, coupling2, near_list, near_count, far0_list, far1_list, far2_list):
    blocks_x = charges.reshape(NRHS, LEAVES, P_SIZE)
    blocks_t = coords.reshape(3, LEAVES, P_SIZE)

    def near_leaf(leaf):
        targets = blocks_t[:, leaf]
        running = jnp.zeros((NRHS, P_SIZE), jnp.float32)
        for k in range(NEAR):
            source = near_list[leaf, k]
            kern = kernel_block(targets, blocks_t[:, source])
            kern = jnp.where(near_count[leaf] > k, kern, 0.0)
            running = running + jnp.dot(blocks_x[:, source], kern.T, precision=highest, preferred_element_type=jnp.float32)
        return running
    near_pot = lax.map(near_leaf, jnp.arange(LEAVES, dtype=jnp.int32))
    near_pot = jnp.transpose(near_pot, (1, 0, 2))
    leaf_basis = basis.reshape(P_SIZE, LEAVES, R)
    up_one = transfer1.reshape(R, LEAVES, R)
    up_two = transfer2.reshape(R, MIDS, R)
    q_leaf = jnp.einsum('nlp,pla->nla', blocks_x, leaf_basis, precision=highest)
    q_mid = jnp.einsum('nla,alb->nlb', q_leaf, up_one, precision=highest).reshape(NRHS, MIDS, CHILD, R).sum(2)
    q_top = jnp.einsum('nma,amb->nmb', q_mid, up_two, precision=highest).reshape(NRHS, TOPS, MIDS_TOP, R).sum(2)
    couple_two = coupling2.reshape(FAR2, R, TOPS, R)
    y_top = jnp.einsum('ntfa,fatb->ntb', q_top[:, far2_list], couple_two, precision=highest)
    couple_one = coupling1.reshape(FAR1, R, MIDS, R)
    y_mid = jnp.einsum('nmfa,famb->nmb', q_mid[:, far1_list], couple_one, precision=highest)
    y_mid = y_mid + jnp.einsum('nmb,amb->nma', jnp.repeat(y_top, MIDS_TOP, axis=1), up_two, precision=highest)
    couple_zero = coupling0.reshape(FAR0, R, LEAVES, R)
    y_leaf = jnp.einsum('nlfa,falb->nlb', q_leaf[:, far0_list], couple_zero, precision=highest)
    y_leaf = y_leaf + jnp.einsum('nlb,alb->nla', jnp.repeat(y_mid, CHILD, axis=1), up_one, precision=highest)
    far_pot = jnp.einsum('nla,pla->nlp', y_leaf, leaf_basis, precision=highest)
    return (near_pot + far_pot).reshape(NRHS, POINTS)
```

```python
import math

import jax
import jax.numpy as jnp
from jax import lax
from jax.experimental import pallas as pl
from jax.experimental.pallas import tpu as pltpu
from jax.sharding import PartitionSpec as P

AXES = ("grp", "lane")
LANES = 8
DEVS = 128
LEAF = 24
MID = 6
PTS = 256
RANK = 64
NEAR = 9
FAR0 = 8
FAR1 = 4
FAR2 = 4
UNROLL = 12
LIST = 256
inv_four_pi = 1.0 / (4.0 * math.pi)
smooth_sq = 5e-05
bf16 = jnp.bfloat16
f32 = jnp.float32
NT = (((1,), (1,)), ((), ()))


def dot(a, b, dims=(((1,), (0,)), ((), ()))):
    return lax.dot_general(a, b, dims, preferred_element_type=f32)


def split(a):
    high = a.astype(bf16)
    return high, (a - high.astype(f32)).astype(bf16)


def lanes_low(shape):
    return lax.broadcasted_iota(jnp.int32, shape, len(shape) - 1) < RANK


def swap_halves(a):
    return pltpu.roll(a, RANK, 1)


def halves(tile):
    low = lanes_low(tile.shape)
    return jnp.where(low, tile, 0.0), jnp.where(low, 0.0, tile)


def place_of():
    return lax.axis_index("grp") * LANES + lax.axis_index("lane")


def relative(entry, place, width):
    rel = lax.rem(entry - place * width + (DEVS + 1) * width, DEVS * width)
    cat = rel // width
    index = rel - cat * width
    other = jnp.where(lax.rem(place, 2) == 0, 2, 0)
    block = jnp.where(cat == 1, 0, jnp.where(cat == other, 1, 2))
    return block, index


def stacked_split(rows_a, rows_b):
    ah, al = split(rows_a)
    bh, bl = split(rows_b)
    return jnp.concatenate([ah, bh, al, bl], axis=0)


def wide_split(a):
    h, l = split(a)
    return jnp.concatenate([h, l], axis=1)


def fold(out):
    s = out[:, :128] + out[:, 128:]
    return s[0:64] + s[128:192], s[64:128] + s[192:256]


def transposed(rows_a, rows_b, weights):
    lhs = stacked_split(rows_a, rows_b)
    wh, wl = split(weights)
    r = dot(lhs, wh, NT)
    r2 = dot(lhs[:128], wl, NT)
    return r[0:64] + r[128:192] + r2[0:64], r[64:128] + r[192:256] + r2[64:128]


def up_kernel(near_ref, count_ref, coords_ref, x_ref, basis_ref, t1_ref, t2_ref, pack_ref, top_ref, list_ref, n_ref):
    place = place_of()
    tiles = []
    for t in range(LEAF // 2):
        xa = x_ref[:, t * 512:t * 512 + 256]
        xb = x_ref[:, t * 512 + 256:t * 512 + 512]
        ra, rb = fold(dot(stacked_split(xa, xb), wide_split(basis_ref[:, t * 128:t * 128 + 128])))
        q = jnp.where(lanes_low(ra.shape), ra, rb)
        pack_ref[t] = q
        tiles.append(q)
    mids = []
    parts = []
    for m in range(MID):
        a0, b0 = halves(tiles[2 * m])
        a1, b1 = halves(tiles[2 * m + 1])
        e0 = t1_ref[:, m * 256:m * 256 + 128]
        e1 = t1_ref[:, m * 256 + 128:m * 256 + 256]
        lhs = stacked_split(jnp.concatenate([a0, a1], axis=1), jnp.concatenate([b0, b1], axis=1))
        parts.append(fold(dot(lhs, wide_split(jnp.concatenate([e0, e0, e1, e1], axis=0)))))
    for t in range(MID // 2):
        (top0, bot0), (top1, bot1) = parts[2 * t], parts[2 * t + 1]
        low = lanes_low(top0.shape)
        mid = jnp.where(low, top0, bot1) + swap_halves(jnp.where(low, top1, bot0))
        pack_ref[LEAF // 2 + t] = mid
        mids.append(mid)
    both = [halves(m) for m in mids]
    weights = [t2_ref[:, t * 128:t * 128 + 128] for t in range(MID // 2)]
    lhs = stacked_split(
        jnp.concatenate([b[0] for b in both], axis=1), jnp.concatenate([b[1] for b in both], axis=1)
    )
    top, bot = fold(dot(lhs, wide_split(jnp.concatenate([w for w in weights for _ in range(2)], axis=0))))
    s = jnp.where(lanes_low(top.shape), top, bot)
    s = s + swap_halves(s)
    top_ref[...] = jnp.where(lanes_low((32, 128)), s[:32], s[32:])
    for i in range(2 * LEAF):
        for c in range(3):
            pack_ref[15 + c, i:i + 1, :] = coords_ref[c:c + 1, i * 128:i * 128 + 128]
    zero = jnp.zeros((16, 128), f32)
    for c in range(3):
        pack_ref[15 + c, 48:64, :] = zero

    def leaf_step(leaf, at):
        live = count_ref[leaf]
        for k in range(NEAR):
            block, index = relative(near_ref[leaf, k], place, LEAF)
            one = jnp.where(live > k, 1, 0)
            pos = jnp.where(block == 0, at[0], jnp.where(block == 1, at[1], at[2]))
            list_ref[2 * block, pos] = leaf
            list_ref[2 * block + 1, pos] = index
            at = tuple(at[b] + jnp.where(block == b, one, 0) for b in range(3))
        return at

    zero = jnp.int32(0)
    at = lax.fori_loop(0, LEAF, leaf_step, (zero, zero, zero))
    for b in range(3):
        n_ref[b] = at[b]
        for u in range(UNROLL):
            list_ref[2 * b, at[b] + u] = LEAF
            list_ref[2 * b + 1, at[b] + u] = 0


def leaf_rows(pack_ref, leaf):
    row = lax.broadcasted_iota(jnp.int32, (8, PTS), 0)
    out = jnp.zeros((8, PTS), f32)
    for c in range(3):
        line = jnp.concatenate(
            [pack_ref[15 + c, 2 * leaf:2 * leaf + 1, :], pack_ref[15 + c, 2 * leaf + 1:2 * leaf + 2, :]], axis=1
        )
        out = jnp.where(row == c, line, out)
    return out


def pieces(a):
    h = a.astype(bf16).astype(f32)
    r = a - h
    m = r.astype(bf16).astype(f32)
    return h, m, r - m


def near_kernel(block, first, last, list_ref, n_ref, own_ref, src_ref, x_ref, *refs):
    if first:
        acc_in = None
        out_ref, targets, centres, feats, xs, acc = refs
    else:
        acc_in, out_ref, targets, centres, feats, xs, acc = refs
    row = lax.broadcasted_iota(jnp.int32, (8, PTS), 0)
    eye = jnp.where(
        lax.broadcasted_iota(jnp.int32, (PTS, PTS), 0) == lax.broadcasted_iota(jnp.int32, (PTS, PTS), 1), 1.0, 0.0
    ).astype(bf16)
    for leaf in range(LEAF):
        targets[leaf] = leaf_rows(own_ref, leaf)
        source = leaf_rows(src_ref, leaf)
        centre = jnp.broadcast_to(jnp.sum(source, axis=1, keepdims=True) * (1.0 / PTS), (8, PTS))
        centres[leaf] = centre
        d = source - centre
        sq = jnp.sum(d * d, axis=0, keepdims=True) + smooth_sq
        h, m, l = pieces(jnp.where(row < 3, -2.0 * d, jnp.where(row == 3, 1.0, jnp.where(row == 4, sq, 0.0))))
        rows = jnp.concatenate([h, m, h, l, m, h, jnp.zeros((80, PTS), f32)], axis=0).astype(bf16)
        feats[leaf] = dot(eye, rows, NT).astype(bf16)
        xh, xl = split(x_ref[:, leaf * PTS:leaf * PTS + PTS] * inv_four_pi)
        xs[leaf] = jnp.concatenate([xh, xl], axis=0)
        if first:
            acc[leaf] = jnp.zeros((64, PTS), f32)
        else:
            acc[leaf] = acc_in[leaf]
    targets[LEAF] = jnp.zeros((8, PTS), f32)
    acc[LEAF] = jnp.zeros((64, PTS), f32)
    unit = jnp.where(row == 4, 1.0, 0.0)

    @pl.loop(0, (n_ref[block] + (UNROLL - 1)) // UNROLL)
    def _(i):
        ls = [list_ref[2 * block, i * UNROLL + u] for u in range(UNROLL)]
        js = [list_ref[2 * block + 1, i * UNROLL + u] for u in range(UNROLL)]
        dist = []
        for l, j in zip(ls, js):
            d = targets[l] - centres[j]
            sq = jnp.sum(d * d, axis=0, keepdims=True)
            h, m, low = pieces(jnp.where(row == 3, sq, d + unit))
            rows = jnp.concatenate([h, h, m, h, m, low], axis=0).astype(bf16)
            dist.append(dot(feats[j][:, :48], rows))
        for l, j, d2 in zip(ls, js, dist):
            kh, kl = split(lax.rsqrt(d2))
            x = xs[j]
            r = dot(x, kh) + dot(x, kl)
            acc[l] += r[:64] + r[64:]

    for leaf in range(LEAF):
        if last:
            out_ref[:, leaf * PTS:leaf * PTS + PTS] = acc[leaf]
        else:
            out_ref[leaf] = acc[leaf]


def far_kernel(
    far0_ref, far1_ref, far2_ref, p0_ref, p1_ref, p2_ref, tops_ref, c0_ref, c1_ref, c2_ref, t1_ref, t2_ref, basis_ref,
    acc_in, out_ref, q_ref,
):
    place = place_of()
    group = lax.axis_index("grp")
    for b, pack in enumerate((p0_ref, p1_ref, p2_ref)):
        for t in range(15):
            h, l = split(pack[t])
            q_ref[b * 15 + t] = jnp.concatenate([h, l], axis=0)

    def picked(tile, parity):
        half = lax.broadcasted_iota(jnp.int32, (128, 128), 1) // RANK
        return jnp.where(half == parity, tile, jnp.zeros_like(tile))

    def coupled(entries, weights):
        lhs = jnp.concatenate(
            [jnp.concatenate([picked(q_ref[tile], parity) for tile, parity in row], axis=1) for row in entries], axis=0
        )
        out = dot(lhs, wide_split(jnp.concatenate([w for w in weights for _ in range(2)], axis=0)))
        s = out[:, :128] + out[:, 128:]
        even, odd = s[0:64] + s[64:128], s[128:192] + s[192:256]
        return jnp.where(lanes_low(even.shape), even, odd)

    def entry(ref, target, f, width, base):
        block, index = relative(ref[target, f], place, width)
        return block * 15 + base + index // 2, lax.rem(index, 2)

    tiles = []
    for f in range(0, FAR2, 2):
        a = tops_ref[far2_ref[group, f]]
        b = tops_ref[far2_ref[group, f + 1]]
        a = jnp.concatenate([a, swap_halves(a)], axis=0)
        b = jnp.concatenate([swap_halves(b), b], axis=0)
        tiles.append(jnp.where(lanes_low(a.shape), a, b))
    th, tl = split(jnp.concatenate(tiles, axis=1))
    w = jnp.concatenate([c2_ref[f] for f in range(FAR2)], axis=0)
    wh, wl = split(jnp.concatenate([w, w], axis=1))
    y2 = dot(th, wh) + dot(tl, wh) + dot(th, wl)

    y1 = []
    for t in range(MID // 2):
        y = coupled(
            [[entry(far1_ref, 2 * t + i, f, MID, 12) for f in range(FAR1)] for i in range(2)],
            [c1_ref[f, :, t * 128:t * 128 + 128] for f in range(FAR1)],
        )
        w = t2_ref[:, t * 128:t * 128 + 128]
        even, odd = transposed(*halves(y2), jnp.concatenate([w, w], axis=0))
        y1.append(y + jnp.where(lanes_low(y.shape), even, odd))

    for t in range(LEAF // 2):
        y = coupled(
            [[entry(far0_ref, 2 * t + i, f, LEAF, 0) for f in range(FAR0)] for i in range(2)],
            [c0_ref[f, :, t * 128:t * 128 + 128] for f in range(FAR0)],
        )
        parent = y1[t // 4]
        other = swap_halves(parent)
        low = lanes_low(parent.shape)
        parent = jnp.where(low, parent, other) if (t // 2) % 2 == 0 else jnp.where(low, other, parent)
        w = t1_ref[:, t * 128:t * 128 + 128]
        even, odd = transposed(*halves(parent), jnp.concatenate([w, w], axis=0))
        y = y + jnp.where(low, even, odd)
        even, odd = transposed(*halves(y), basis_ref[:, t * 128:t * 128 + 128])
        out_ref[2 * t] = acc_in[2 * t] + even
        out_ref[2 * t + 1] = acc_in[2 * t + 1] + odd


VM = pl.BlockSpec(memory_space=pltpu.VMEM)
SM = pl.BlockSpec(memory_space=pltpu.SMEM)
PARAMS = pltpu.CompilerParams(vmem_limit_bytes=48 << 20)


def near_call(block, first, last, lists, counts, own, src, x, acc=None):
    shape = (64, LEAF * PTS) if last else (LEAF, 64, PTS)
    args = (lists, counts, own, src, x) + (() if first else (acc,))
    return pl.pallas_call(
        lambda *refs: near_kernel(block, first, last, *refs),
        out_shape=jax.ShapeDtypeStruct(shape, f32),
        in_specs=[SM, SM] + [VM] * (len(args) - 2),
        out_specs=VM,
        scratch_shapes=[
            pltpu.VMEM((LEAF + 1, 8, PTS), f32),
            pltpu.VMEM((LEAF, 8, PTS), f32),
            pltpu.VMEM((LEAF, PTS, 128), bf16),
            pltpu.VMEM((LEAF, 128, PTS), bf16),
            pltpu.VMEM((LEAF + 1, 64, PTS), f32),
        ],
        compiler_params=PARAMS,
        cost_estimate=pl.CostEstimate(flops=8_000_000_000, bytes_accessed=8_000_000, transcendentals=0),
        name="near_%d" % block,
    )(*args)


def local(
    coords, charges, basis, transfer1, transfer2, coupling0, coupling1, coupling2, near_list, near_count, far0_list,
    far1_list, far2_list,
):
    same_chip = [(i, i ^ 1) for i in range(DEVS)]
    next_chip = [(i, (i + (1 if i % 2 else DEVS - 1)) % DEVS) for i in range(DEVS)]
    x1 = lax.ppermute(charges, AXES, same_chip)
    x2 = lax.ppermute(charges, AXES, next_chip)
    pack, top, lists, counts = pl.pallas_call(
        up_kernel,
        out_shape=(
            jax.ShapeDtypeStruct((18, 64, 128), f32),
            jax.ShapeDtypeStruct((32, 128), f32),
            jax.ShapeDtypeStruct((6, LIST), jnp.int32),
            jax.ShapeDtypeStruct((4,), jnp.int32),
        ),
        in_specs=[SM, SM] + [VM] * 5,
        out_specs=(VM, VM, SM, SM),
        compiler_params=PARAMS,
        cost_estimate=pl.CostEstimate(flops=1_000_000_000, bytes_accessed=5_000_000, transcendentals=0),
        name="upward",
    )(near_list, near_count, coords, charges, basis, transfer1, transfer2)
    p1 = lax.ppermute(pack, AXES, same_chip)
    p2 = lax.ppermute(pack, AXES, next_chip)
    tops = lax.all_gather(lax.psum(top, "lane"), "grp", axis=0, tiled=False)
    acc = near_call(0, True, False, lists, counts, pack, pack, charges)
    acc = near_call(1, False, False, lists, counts, pack, p1, x1, acc)
    acc = pl.pallas_call(
        far_kernel,
        out_shape=jax.ShapeDtypeStruct((LEAF, 64, PTS), f32),
        in_specs=[SM] * 3 + [VM] * 11,
        out_specs=VM,
        scratch_shapes=[pltpu.VMEM((45, 128, 128), bf16)],
        compiler_params=PARAMS,
        cost_estimate=pl.CostEstimate(flops=3_000_000_000, bytes_accessed=10_000_000, transcendentals=0),
        name="downward",
    )(
        far0_list, far1_list, far2_list, pack, p1, p2, tops, coupling0, coupling1, coupling2, transfer1, transfer2,
        basis, acc,
    )
    return near_call(2, False, True, lists, counts, pack, p2, x2, acc)


def solution(mesh):
    placed = (
        P(None, AXES),
        P(None, AXES),
        P(None, AXES),
        P(None, AXES),
        P(None, AXES),
        P(None, None, AXES),
        P(None, None, AXES),
        P(None, None, "grp"),
        P(AXES, None),
        P(AXES),
        P(AXES, None),
        P(AXES, None),
        P(),
    )
    return jax.shard_map(local, mesh=mesh, in_specs=placed, out_specs=P(None, AXES), check_vma=False)
```

```python
import math

import jax
import jax.numpy as jnp
from jax import lax
from jax.experimental import pallas as pl
from jax.experimental.pallas import tpu as pltpu
from jax.sharding import PartitionSpec as P

AXES = ("grp", "lane")
LANES = 8
DEVS = 128
LEAF = 24
MID = 6
PTS = 256
RANK = 64
NEAR = 9
FAR0 = 8
FAR1 = 4
FAR2 = 4
UNROLL = 12
LIST = 512
SLOTS = 5
COUNT_AT = 127
REST_AT = 128
GROUPS = 16
MESH = pl.DeviceIdType.MESH
inv_four_pi = 1.0 / (4.0 * math.pi)
smooth_sq = 5e-05
bf16 = jnp.bfloat16
f32 = jnp.float32
NT = (((1,), (1,)), ((), ()))


def dot(a, b, dims=(((1,), (0,)), ((), ()))):
    return lax.dot_general(a, b, dims, preferred_element_type=f32)


def split(a):
    high = a.astype(bf16)
    return high, (a - high.astype(f32)).astype(bf16)


def lanes_low(shape):
    return lax.broadcasted_iota(jnp.int32, shape, len(shape) - 1) < RANK


def swap_halves(a):
    return pltpu.roll(a, RANK, 1)


def halves(tile):
    low = lanes_low(tile.shape)
    return jnp.where(low, tile, 0.0), jnp.where(low, 0.0, tile)


def place_of():
    return lax.axis_index("grp") * LANES + lax.axis_index("lane")


def relative(entry, place, width):
    rel = lax.rem(entry - place * width + (DEVS + 1) * width, DEVS * width)
    cat = rel // width
    index = rel - cat * width
    other = jnp.where(lax.rem(place, 2) == 0, 2, 0)
    block = jnp.where(cat == 1, 0, jnp.where(cat == other, 1, 2))
    return block, index


def stacked_split(rows_a, rows_b):
    ah, al = split(rows_a)
    bh, bl = split(rows_b)
    return jnp.concatenate([ah, bh, al, bl], axis=0)


def wide_split(a):
    h, l = split(a)
    return jnp.concatenate([h, l], axis=1)


def fold(out):
    s = out[:, :128] + out[:, 128:]
    return s[0:64] + s[128:192], s[64:128] + s[192:256]


def transposed(rows_a, rows_b, weights):
    lhs = stacked_split(rows_a, rows_b)
    wh, wl = split(weights)
    r = dot(lhs, wh, NT)
    r2 = dot(lhs[:128], wl, NT)
    return r[0:64] + r[128:192] + r2[0:64], r[64:128] + r[192:256] + r2[64:128]


def list_kernel(near_ref, count_ref, list_ref):
    place = place_of()
    even = lax.rem(place, 2) == 0
    low_off = jnp.where(even, 72, 48)
    high_off = jnp.where(even, 0, 24)

    def leaf_step(leaf, pos):
        live = count_ref[leaf]
        list_ref[leaf * SLOTS] = leaf
        for s in range(1, SLOTS):
            list_ref[leaf * SLOTS + s] = LEAF
        own_at = leaf * SLOTS + 1
        own_end = leaf * SLOTS + SLOTS
        for k in range(1, NEAR):
            rel = near_ref[leaf, k] - place * LEAF
            rel = jnp.where(rel < -LEAF, rel + DEVS * LEAF, jnp.where(rel >= 2 * LEAF, rel - DEVS * LEAF, rel))
            near_side = jnp.logical_and(rel >= 0, rel < LEAF)
            source = rel + jnp.where(near_side, 0, jnp.where(rel < 0, low_off, high_off))
            here = jnp.logical_and(jnp.logical_and(near_side, own_at < own_end), live > k)
            list_ref[jnp.where(here, own_at, REST_AT + pos)] = jnp.where(here, source, leaf * 128 + source)
            own_at = own_at + jnp.where(here, 1, 0)
            pos = pos + jnp.where(jnp.logical_and(live > k, jnp.logical_not(here)), 1, 0)
        return pos

    pos = lax.fori_loop(0, LEAF, leaf_step, jnp.int32(0))
    list_ref[COUNT_AT] = pos
    for u in range(UNROLL):
        list_ref[REST_AT + pos + u] = LEAF * 128


def upward(coords_ref, x_ref, basis_ref, t1_ref, t2_ref, pack_ref):
    tiles = []
    for t in range(LEAF // 2):
        xa = x_ref[:, t * 512:t * 512 + 256]
        xb = x_ref[:, t * 512 + 256:t * 512 + 512]
        ra, rb = fold(dot(stacked_split(xa, xb), wide_split(basis_ref[:, t * 128:t * 128 + 128])))
        q = jnp.where(lanes_low(ra.shape), ra, rb)
        pack_ref[t] = q
        tiles.append(q)
    mids = []
    parts = []
    for m in range(MID):
        a0, b0 = halves(tiles[2 * m])
        a1, b1 = halves(tiles[2 * m + 1])
        e0 = t1_ref[:, m * 256:m * 256 + 128]
        e1 = t1_ref[:, m * 256 + 128:m * 256 + 256]
        lhs = stacked_split(jnp.concatenate([a0, a1], axis=1), jnp.concatenate([b0, b1], axis=1))
        parts.append(fold(dot(lhs, wide_split(jnp.concatenate([e0, e0, e1, e1], axis=0)))))
    for t in range(MID // 2):
        (top0, bot0), (top1, bot1) = parts[2 * t], parts[2 * t + 1]
        low = lanes_low(top0.shape)
        mid = jnp.where(low, top0, bot1) + swap_halves(jnp.where(low, top1, bot0))
        pack_ref[LEAF // 2 + t] = mid
        mids.append(mid)
    both = [halves(m) for m in mids]
    weights = [t2_ref[:, t * 128:t * 128 + 128] for t in range(MID // 2)]
    lhs = stacked_split(
        jnp.concatenate([b[0] for b in both], axis=1), jnp.concatenate([b[1] for b in both], axis=1)
    )
    top, bot = fold(dot(lhs, wide_split(jnp.concatenate([w for w in weights for _ in range(2)], axis=0))))
    for i in range(2 * LEAF):
        for c in range(3):
            pack_ref[15 + c, i:i + 1, :] = coords_ref[c:c + 1, i * 128:i * 128 + 128]
    zero = jnp.zeros((16, 128), f32)
    for c in range(3):
        pack_ref[15 + c, 48:64, :] = zero
    s = jnp.where(lanes_low(top.shape), top, bot)
    return s + swap_halves(s)


def leaf_rows(pack_ref, leaf):
    row = lax.broadcasted_iota(jnp.int32, (8, PTS), 0)
    out = jnp.zeros((8, PTS), f32)
    for c in range(3):
        line = jnp.concatenate(
            [pack_ref[15 + c, 2 * leaf:2 * leaf + 1, :], pack_ref[15 + c, 2 * leaf + 1:2 * leaf + 2, :]], axis=1
        )
        out = jnp.where(row == c, line, out)
    return out


def pieces(a):
    h = a.astype(bf16).astype(f32)
    r = a - h
    m = r.astype(bf16).astype(f32)
    return h, m, r - m


def identity():
    return jnp.where(
        lax.broadcasted_iota(jnp.int32, (PTS, PTS), 0) == lax.broadcasted_iota(jnp.int32, (PTS, PTS), 1), 1.0, 0.0
    ).astype(bf16)


def prepare(pack_ref, x_ref, leaf, at, eye, centres, feats, xs):
    row = lax.broadcasted_iota(jnp.int32, (8, PTS), 0)
    source = leaf_rows(pack_ref, leaf)
    centre = jnp.broadcast_to(jnp.sum(source, axis=1, keepdims=True) * (1.0 / PTS), (8, PTS))
    centres[at] = centre
    d = source - centre
    sq = jnp.sum(d * d, axis=0, keepdims=True) + smooth_sq
    h, m, l = pieces(jnp.where(row < 3, -2.0 * d, jnp.where(row == 3, 1.0, jnp.where(row == 4, sq, 0.0))))
    rows = jnp.concatenate([h, m, h, l, m, h, jnp.zeros((80, PTS), f32)], axis=0).astype(bf16)
    feats[at] = dot(eye, rows, NT).astype(bf16)
    xh, xl = split(x_ref[:, leaf * PTS:leaf * PTS + PTS] * inv_four_pi)
    xs[at] = jnp.concatenate([xh, xl], axis=0)


def pairs(ls, js, targets, centres, feats, xs, acc):
    unit = jnp.where(lax.broadcasted_iota(jnp.int32, (8, PTS), 0) == 4, 1.0, 0.0)
    row = lax.broadcasted_iota(jnp.int32, (8, PTS), 0)
    dist = []
    for l, j in zip(ls, js):
        d = targets[l] - centres[j]
        sq = jnp.sum(d * d, axis=0, keepdims=True)
        h, m, low = pieces(jnp.where(row == 3, sq, d + unit))
        rows = jnp.concatenate([h, h, m, h, m, low], axis=0).astype(bf16)
        dist.append(dot(feats[j][:, :48], rows))
    for l, j, d2 in zip(ls, js, dist):
        kh, kl = split(lax.rsqrt(d2))
        x = xs[j]
        r = dot(x, kh) + dot(x, kl)
        acc[l] += r[:64] + r[64:]


def first_kernel(
    list_ref, far2_ref, coords_hbm, x_hbm, basis_hbm, t1_hbm, t2_hbm, c2_ref,
    acc_ref, pack_ref, p1_ref, p2_ref, x1_ref, x2_ref, y2_ref, centres, feats, xs,
    coords, x, basis, t1, t2, targets, parts, parts_in, mine, slices, y2_mine, y2_in,
    load_sem, part_send, part_recv, slice_send, slice_recv, y2_send, y2_recv, near_send, near_recv,
):
    group = lax.axis_index("grp")
    lane = lax.axis_index("lane")
    place = group * LANES + lane
    even = lax.rem(lane, 2) == 0
    partner = (group, lane + 1 - 2 * lax.rem(lane, 2))
    beyond = lax.rem(place + jnp.where(even, DEVS - 1, 1), DEVS)
    beyond = (beyond // LANES, lax.rem(beyond, LANES))
    loads = [
        pltpu.make_async_copy(src, dst, load_sem.at[i])
        for i, (src, dst) in enumerate(
            [(x_hbm.at[:, c * 1536:c * 1536 + 1536], x.at[:, c * 1536:c * 1536 + 1536]) for c in range(4)]
            + [(basis_hbm.at[r * 64:r * 64 + 64], basis.at[r * 64:r * 64 + 64]) for r in range(4)]
            + [(t1_hbm, t1), (t2_hbm, t2), (coords_hbm, coords)]
        )
    ]
    for c in loads:
        c.start()
    barrier = pltpu.get_barrier_semaphore()
    for d in range(1, LANES):
        pl.semaphore_signal(barrier, inc=1, device_id=(group, lax.rem(lane + d, LANES)), device_id_type=MESH)
    for d in range(1, GROUPS):
        pl.semaphore_signal(barrier, inc=1, device_id=(lax.rem(group + d, GROUPS), lane), device_id_type=MESH)
    pl.semaphore_signal(barrier, inc=1, device_id=beyond, device_id_type=MESH)
    for c in loads:
        c.wait()
    top = upward(coords, x, basis, t1, t2, pack_ref)
    for r in range(LANES):
        parts[r] = top[r * 8:r * 8 + 8]
    pl.semaphore_wait(barrier, LANES + GROUPS - 1)

    def part_copy(d):
        peer = lax.rem(lane + d, LANES)
        return pltpu.make_async_remote_copy(
            parts.at[peer], parts_in.at[lane], part_send.at[d], part_recv.at[lane], (group, peer), MESH
        ), pltpu.make_async_remote_copy(
            parts.at[peer], parts_in.at[peer], part_send.at[d], part_recv.at[peer], (group, peer), MESH
        )

    def slice_copy(d):
        peer = lax.rem(group + d, GROUPS)
        return pltpu.make_async_remote_copy(
            mine, slices.at[group], slice_send.at[d], slice_recv.at[group], (peer, lane), MESH
        ), pltpu.make_async_remote_copy(
            mine, slices.at[peer], slice_send.at[d], slice_recv.at[peer], (peer, lane), MESH
        )

    def y2_copy(d):
        peer = lax.rem(lane + d, LANES)
        return pltpu.make_async_remote_copy(
            y2_mine, y2_in.at[lane], y2_send.at[d], y2_recv.at[lane], (group, peer), MESH
        ), pltpu.make_async_remote_copy(
            y2_mine, y2_in.at[peer], y2_send.at[d], y2_recv.at[peer], (group, peer), MESH
        )

    for d in range(1, LANES):
        part_copy(d)[0].start()
    swaps = [
        pltpu.make_async_remote_copy(src, dst, near_send.at[i], near_recv.at[i], dev, MESH)
        for i, (src, dst, dev) in enumerate(
            [(pack_ref, p2_ref, beyond), (pack_ref, p1_ref, partner), (x_hbm, x1_ref, partner)]
        )
    ]
    back = pltpu.make_async_remote_copy(x_hbm, x2_ref, near_send.at[3], near_recv.at[3], beyond, MESH)
    for c in swaps:
        c.start()

    @pl.when(even)
    def _():
        back.start()

    eye = identity()
    for leaf in range(LEAF):
        targets[leaf] = leaf_rows(pack_ref, leaf)
        prepare(pack_ref, x, leaf, leaf, eye, centres, feats, xs)
        acc_ref[leaf] = jnp.zeros((64, PTS), f32)
    centres[LEAF] = jnp.zeros((8, PTS), f32)
    feats[LEAF] = feats[0]
    xs[LEAF] = jnp.zeros((128, PTS), bf16)

    def leaves(i, _):
        ls = [2 * i + u for u in range(2) for s in range(SLOTS)]
        js = [list_ref[(2 * i + u) * SLOTS + s] for u in range(2) for s in range(SLOTS)]
        pairs(ls, js, targets, centres, feats, xs, acc_ref)
        return 0

    for d in range(1, LANES):
        part_copy(d)[1].wait_recv()
    parts_in[lane] = parts[lane]
    total = parts_in[0]
    for r in range(1, LANES):
        total = total + parts_in[r]
    mine[...] = total
    slices[group] = total
    for d in range(1, GROUPS):
        slice_copy(d)[0].start()

    lax.fori_loop(0, 4, leaves, 0)

    for d in range(1, GROUPS):
        slice_copy(d)[1].wait_recv()
    low = lanes_low((8, 128))
    picks = [slices[far2_ref[group, f]] for f in range(FAR2)]
    rows = jnp.concatenate([jnp.where(low, picks[f], picks[f + 1]) for f in range(0, FAR2, 2)], axis=1)
    w = jnp.concatenate([c2_ref[f] for f in range(FAR2)], axis=0)
    wh, wl = split(jnp.concatenate([w, w], axis=1))
    rh, rl = split(rows)
    y2 = dot(rh, wh) + dot(rl, wh) + dot(rh, wl)
    y2_mine[...] = y2
    y2_in[lane] = y2
    for d in range(1, LANES):
        y2_copy(d)[0].start()

    lax.fori_loop(4, LEAF // 2, leaves, 0)

    for d in range(1, LANES):
        y2_copy(d)[1].wait_recv()
    for r in range(LANES):
        y2_ref[r * 8:r * 8 + 8, :] = y2_in[r]
    for d in range(1, LANES):
        part_copy(d)[0].wait_send()
        y2_copy(d)[0].wait_send()
    for d in range(1, GROUPS):
        slice_copy(d)[0].wait_send()
    for c in swaps:
        c.wait()

    @pl.when(even)
    def _():
        back.wait_send()

    @pl.when(jnp.logical_not(even))
    def _():
        back.wait_recv()


def rest_kernel(
    list_ref, own_ref, p1_ref, p2_ref, own_centres, own_feats, own_xs, x1_hbm, x2_hbm, x3_hbm, acc_in, out_ref,
    targets, centres, feats, xs, acc, x, sem,
):
    even = lax.rem(lax.axis_index("lane"), 2) == 0

    def load(src, i):
        return pltpu.make_async_copy(src, x.at[i], sem.at[i])

    load(x1_hbm, 0).start()

    @pl.when(even)
    def _():
        load(x3_hbm, 1).start()

    @pl.when(jnp.logical_not(even))
    def _():
        load(x2_hbm, 1).start()

    moves = [
        pltpu.make_async_copy(own_feats.at[0:LEAF], feats.at[0:LEAF], sem.at[2]),
        pltpu.make_async_copy(own_xs.at[0:LEAF], xs.at[0:LEAF], sem.at[3]),
    ]
    for c in moves:
        c.start()
    for leaf in range(LEAF):
        targets[leaf] = leaf_rows(own_ref, leaf)
        centres[leaf] = own_centres[leaf]
        acc[leaf] = acc_in[leaf]
    targets[LEAF] = jnp.zeros((8, PTS), f32)
    acc[LEAF] = jnp.zeros((64, PTS), f32)
    eye = identity()
    for b, pack in enumerate((p1_ref, p2_ref)):
        load(x1_hbm, b).wait()
        for leaf in range(LEAF):
            prepare(pack, x.at[b], leaf, LEAF * (b + 1) + leaf, eye, centres, feats, xs)
    for c in moves:
        c.wait()

    @pl.loop(0, (list_ref[COUNT_AT] + (UNROLL - 1)) // UNROLL)
    def _(i):
        words = [list_ref[REST_AT + i * UNROLL + u] for u in range(UNROLL)]
        pairs([w // 128 for w in words], [lax.rem(w, 128) for w in words], targets, centres, feats, xs, acc)

    for leaf in range(LEAF):
        out_ref[:, leaf * PTS:leaf * PTS + PTS] = acc[leaf]


def far_kernel(
    far0_ref, far1_ref, p0_ref, p1_ref, p2_ref, y2_ref, c0_ref, c1_ref, t1_ref, t2_ref, basis_ref,
    acc_in, out_ref, q_ref,
):
    place = place_of()
    for b, pack in enumerate((p0_ref, p1_ref, p2_ref)):
        for t in range(15):
            h, l = split(pack[t])
            q_ref[b * 15 + t] = jnp.concatenate([h, l], axis=0)

    def picked(tile, parity):
        half = lax.broadcasted_iota(jnp.int32, (128, 128), 1) // RANK
        return jnp.where(half == parity, tile, jnp.zeros_like(tile))

    def coupled(entries, weights):
        lhs = jnp.concatenate(
            [jnp.concatenate([picked(q_ref[tile], parity) for tile, parity in row], axis=1) for row in entries], axis=0
        )
        out = dot(lhs, wide_split(jnp.concatenate([w for w in weights for _ in range(2)], axis=0)))
        s = out[:, :128] + out[:, 128:]
        even, odd = s[0:64] + s[64:128], s[128:192] + s[192:256]
        return jnp.where(lanes_low(even.shape), even, odd)

    def entry(ref, target, f, width, base):
        block, index = relative(ref[target, f], place, width)
        return block * 15 + base + index // 2, lax.rem(index, 2)

    y2 = y2_ref[...]
    y1 = []
    for t in range(MID // 2):
        y = coupled(
            [[entry(far1_ref, 2 * t + i, f, MID, 12) for f in range(FAR1)] for i in range(2)],
            [c1_ref[f, :, t * 128:t * 128 + 128] for f in range(FAR1)],
        )
        w = t2_ref[:, t * 128:t * 128 + 128]
        even, odd = transposed(*halves(y2), jnp.concatenate([w, w], axis=0))
        y1.append(y + jnp.where(lanes_low(y.shape), even, odd))

    for t in range(LEAF // 2):
        y = coupled(
            [[entry(far0_ref, 2 * t + i, f, LEAF, 0) for f in range(FAR0)] for i in range(2)],
            [c0_ref[f, :, t * 128:t * 128 + 128] for f in range(FAR0)],
        )
        parent = y1[t // 4]
        other = swap_halves(parent)
        low = lanes_low(parent.shape)
        parent = jnp.where(low, parent, other) if (t // 2) % 2 == 0 else jnp.where(low, other, parent)
        w = t1_ref[:, t * 128:t * 128 + 128]
        even, odd = transposed(*halves(parent), jnp.concatenate([w, w], axis=0))
        y = y + jnp.where(low, even, odd)
        even, odd = transposed(*halves(y), basis_ref[:, t * 128:t * 128 + 128])
        out_ref[2 * t] = acc_in[2 * t] + even
        out_ref[2 * t + 1] = acc_in[2 * t + 1] + odd


VM = pl.BlockSpec(memory_space=pltpu.VMEM)
SM = pl.BlockSpec(memory_space=pltpu.SMEM)
ANY = pl.BlockSpec(memory_space=pl.ANY)
DMA = pltpu.SemaphoreType.DMA


def params(mib, **more):
    return pltpu.CompilerParams(vmem_limit_bytes=mib << 20, **more)


def cost(size):
    return pl.CostEstimate(flops=size, bytes_accessed=1000, transcendentals=0)


def shape(*dims, dtype=f32):
    return jax.ShapeDtypeStruct(dims, dtype)


def local(
    coords, charges, basis, transfer1, transfer2, coupling0, coupling1, coupling2, near_list, near_count, far0_list,
    far1_list, far2_list,
):
    x3 = lax.ppermute(charges, AXES, [(i, (i + 1) % DEVS) for i in range(1, DEVS, 2)])
    lists = pl.pallas_call(
        list_kernel, out_shape=shape(LIST, dtype=jnp.int32), in_specs=[SM, SM], out_specs=SM, cost_estimate=cost(1000),
        name="lists",
    )(near_list, near_count)
    acc, pack, p1, p2, x1, x2, y2, centres, feats, xs = pl.pallas_call(
        first_kernel,
        out_shape=(
            shape(LEAF, 64, PTS), shape(18, 64, 128), shape(18, 64, 128), shape(18, 64, 128), shape(64, LEAF * PTS),
            shape(64, LEAF * PTS), shape(64, 128), shape(LEAF + 1, 8, PTS), shape(LEAF + 1, PTS, 128, dtype=bf16),
            shape(LEAF + 1, 128, PTS, dtype=bf16),
        ),
        in_specs=[SM, SM] + [ANY] * 5 + [VM],
        out_specs=(VM, VM, ANY, ANY, ANY, ANY, VM, VM, VM, VM),
        scratch_shapes=[
            pltpu.VMEM((3, LEAF * PTS), f32), pltpu.VMEM((64, LEAF * PTS), f32), pltpu.VMEM((PTS, LEAF * RANK), f32),
            pltpu.VMEM((RANK, LEAF * RANK), f32), pltpu.VMEM((RANK, MID * RANK), f32),
            pltpu.VMEM((LEAF, 8, PTS), f32), pltpu.VMEM((LANES, 8, 128), f32), pltpu.VMEM((LANES, 8, 128), f32),
            pltpu.VMEM((8, 128), f32), pltpu.VMEM((GROUPS, 8, 128), f32), pltpu.VMEM((8, 128), f32),
            pltpu.VMEM((LANES, 8, 128), f32),
            DMA((11,)), DMA((LANES,)), DMA((LANES,)), DMA((GROUPS,)), DMA((GROUPS,)), DMA((LANES,)), DMA((LANES,)),
            DMA((4,)), DMA((4,)),
        ],
        compiler_params=params(24, collective_id=0, has_side_effects=True),
        cost_estimate=cost(1000),
        name="first",
    )(lists, far2_list, coords, charges, basis, transfer1, transfer2, coupling2)
    acc = pl.pallas_call(
        far_kernel,
        out_shape=shape(LEAF, 64, PTS),
        in_specs=[SM] * 2 + [VM] * 10,
        out_specs=VM,
        scratch_shapes=[pltpu.VMEM((45, 128, 128), bf16)],
        compiler_params=params(24),
        cost_estimate=cost(1000),
        name="downward",
    )(far0_list, far1_list, pack, p1, p2, y2, coupling0, coupling1, transfer1, transfer2, basis, acc)
    return pl.pallas_call(
        rest_kernel,
        out_shape=shape(64, LEAF * PTS),
        in_specs=[SM] + [VM] * 4 + [ANY] * 5 + [VM],
        out_specs=VM,
        scratch_shapes=[
            pltpu.VMEM((LEAF + 1, 8, PTS), f32), pltpu.VMEM((3 * LEAF, 8, PTS), f32),
            pltpu.VMEM((3 * LEAF, PTS, 128), bf16), pltpu.VMEM((3 * LEAF, 128, PTS), bf16),
            pltpu.VMEM((LEAF + 1, 64, PTS), f32), pltpu.VMEM((2, 64, LEAF * PTS), f32), DMA((4,)),
        ],
        compiler_params=params(32),
        cost_estimate=cost(1000),
        name="rest",
    )(lists, pack, p1, p2, centres, feats, xs, x1, x2, x3, acc)


def solution(mesh):
    placed = (
        P(None, AXES),
        P(None, AXES),
        P(None, AXES),
        P(None, AXES),
        P(None, AXES),
        P(None, None, AXES),
        P(None, None, AXES),
        P(None, None, "grp"),
        P(AXES, None),
        P(AXES),
        P(AXES, None),
        P(AXES, None),
        P(),
    )
    return jax.shard_map(local, mesh=mesh, in_specs=placed, out_specs=P(None, AXES), check_vma=False)
```

```python
import math

import jax
import jax.numpy as jnp
from jax import lax
from jax.experimental import pallas as pl
from jax.experimental.pallas import tpu as pltpu
from jax.sharding import PartitionSpec as P

AXES = ("grp", "lane")
LANES = 8
DEVS = 128
LEAF = 24
MID = 6
PTS = 256
RANK = 64
NEAR = 9
FAR0 = 8
FAR1 = 4
FAR2 = 4
UNROLL = 18
SLOTS = 5
REST_ROW = 8
COUNT_ROW = 9
CHUNK = 512
GROUPS = 16
MESH = pl.DeviceIdType.MESH
inv_four_pi = 1.0 / (4.0 * math.pi)
smooth_sq = 5e-05
bf16 = jnp.bfloat16
f32 = jnp.float32
NT = (((1,), (1,)), ((), ()))


def dot(a, b, dims=(((1,), (0,)), ((), ()))):
    return lax.dot_general(a, b, dims, preferred_element_type=f32)


def split(a):
    high = a.astype(bf16)
    return high, (a - high.astype(f32)).astype(bf16)


def lanes_low(shape):
    return lax.broadcasted_iota(jnp.int32, shape, len(shape) - 1) < RANK


def swap_halves(a):
    return pltpu.roll(a, RANK, 1)


def halves(tile):
    low = lanes_low(tile.shape)
    return jnp.where(low, tile, 0.0), jnp.where(low, 0.0, tile)


def place_of():
    return lax.axis_index("grp") * LANES + lax.axis_index("lane")


def source_of(entry, place, width):
    even = lax.rem(place, 2) == 0
    rel = entry - place * width
    rel = jnp.where(rel < -width, rel + DEVS * width, jnp.where(rel >= 2 * width, rel - DEVS * width, rel))
    low_off = jnp.where(even, 3 * width, 2 * width)
    high_off = jnp.where(even, 0, width)
    source = rel + jnp.where(rel < 0, low_off, jnp.where(rel >= width, high_off, 0))
    return jnp.minimum(jnp.maximum(source, 0), 3 * width - 1)


def stacked_split(rows_a, rows_b):
    ah, al = split(rows_a)
    bh, bl = split(rows_b)
    return jnp.concatenate([ah, bh, al, bl], axis=0)


def wide_split(a):
    h, l = split(a)
    return jnp.concatenate([h, l], axis=1)


def fold(out):
    s = out[:, :128] + out[:, 128:]
    return s[0:64] + s[128:192], s[64:128] + s[192:256]


def transposed(rows_a, rows_b, weights):
    lhs = stacked_split(rows_a, rows_b)
    wh, wl = split(weights)
    r = dot(lhs, wh, NT)
    r2 = dot(lhs[:128], wl, NT)
    return r[0:64] + r[128:192] + r2[0:64], r[64:128] + r[192:256] + r2[64:128]


def list_kernel(near_ref, count_ref, out_ref):
    place = place_of()
    source = source_of(near_ref[...], place, LEAF)
    count = count_ref[...]
    leaf = lax.broadcasted_iota(jnp.int32, (1, LEAF), 1)
    own_at = jnp.zeros((1, LEAF), jnp.int32)
    rest_at = jnp.zeros((1, LEAF), jnp.int32)
    own = [jnp.full((1, LEAF), LEAF, jnp.int32) for _ in range(SLOTS - 1)]
    places = []
    for k in range(1, NEAR):
        src = source[k:k + 1]
        live = count > k
        here = jnp.logical_and(jnp.logical_and(src < LEAF, live), own_at < SLOTS - 1)
        for s in range(SLOTS - 1):
            own[s] = jnp.where(jnp.logical_and(here, own_at == s), src, own[s])
        own_at = own_at + jnp.where(here, 1, 0)
        rest = jnp.logical_and(live, jnp.logical_not(here))
        places.append((rest, rest_at))
        rest_at = rest_at + jnp.where(rest, 1, 0)
    row = lax.broadcasted_iota(jnp.int32, (LEAF, LEAF), 0)
    col = lax.broadcasted_iota(jnp.int32, (LEAF, LEAF), 1)
    before = jnp.where(row < col, 1.0, 0.0).astype(bf16)
    counts = jnp.broadcast_to(rest_at.astype(f32), (16, LEAF)).astype(bf16)
    base = dot(counts, before)[0:1]
    at = [jnp.where(rest, base + pos.astype(f32), -1.0) for rest, pos in places]
    values = jnp.concatenate(at + [source[k:k + 1].astype(f32) for k in range(1, NEAR)], axis=0).astype(bf16)
    columns = dot(jnp.where(row == col, 1.0, 0.0).astype(bf16), values, NT)
    lanes = lax.broadcasted_iota(jnp.int32, (LEAF, PTS), 1).astype(f32)
    word = lax.broadcasted_iota(jnp.int32, (LEAF, 1), 0).astype(f32) * 128.0
    flat = jnp.zeros((LEAF, PTS), f32)
    for k in range(NEAR - 1):
        flat = flat + jnp.where(columns[:, k:k + 1] == lanes, word + columns[:, NEAR - 1 + k:NEAR + k], 0.0)
    flat = jnp.sum(flat, axis=0, keepdims=True)
    total = jnp.sum(rest_at.astype(f32), axis=1, keepdims=True)
    flat = jnp.where(lanes[0:1] < total, flat, LEAF * 128.0)
    out_ref[...] = jnp.zeros((16, PTS), jnp.int32)
    out_ref[0:1, 0:LEAF] = leaf
    for s in range(SLOTS - 1):
        out_ref[s + 1:s + 2, 0:LEAF] = own[s]
    out_ref[REST_ROW:REST_ROW + 1, :] = flat.astype(jnp.int32)
    out_ref[COUNT_ROW:COUNT_ROW + 1, :] = jnp.broadcast_to(total, (1, PTS)).astype(jnp.int32)


def upward(coords_ref, x_ref, basis_ref, t1_ref, t2_ref, pack_ref):
    tiles = []
    for t in range(LEAF // 2):
        xa = x_ref[:, t * 512:t * 512 + 256]
        xb = x_ref[:, t * 512 + 256:t * 512 + 512]
        ra, rb = fold(dot(stacked_split(xa, xb), wide_split(basis_ref[:, t * 128:t * 128 + 128])))
        q = jnp.where(lanes_low(ra.shape), ra, rb)
        pack_ref[t] = q
        tiles.append(q)
    mids = []
    parts = []
    for m in range(MID):
        a0, b0 = halves(tiles[2 * m])
        a1, b1 = halves(tiles[2 * m + 1])
        e0 = t1_ref[:, m * 256:m * 256 + 128]
        e1 = t1_ref[:, m * 256 + 128:m * 256 + 256]
        lhs = stacked_split(jnp.concatenate([a0, a1], axis=1), jnp.concatenate([b0, b1], axis=1))
        parts.append(fold(dot(lhs, wide_split(jnp.concatenate([e0, e0, e1, e1], axis=0)))))
    for t in range(MID // 2):
        (top0, bot0), (top1, bot1) = parts[2 * t], parts[2 * t + 1]
        low = lanes_low(top0.shape)
        mid = jnp.where(low, top0, bot1) + swap_halves(jnp.where(low, top1, bot0))
        pack_ref[LEAF // 2 + t] = mid
        mids.append(mid)
    both = [halves(m) for m in mids]
    weights = [t2_ref[:, t * 128:t * 128 + 128] for t in range(MID // 2)]
    lhs = stacked_split(
        jnp.concatenate([b[0] for b in both], axis=1), jnp.concatenate([b[1] for b in both], axis=1)
    )
    top, bot = fold(dot(lhs, wide_split(jnp.concatenate([w for w in weights for _ in range(2)], axis=0))))
    for i in range(2 * LEAF):
        for c in range(3):
            pack_ref[15 + c, i:i + 1, :] = coords_ref[c:c + 1, i * 128:i * 128 + 128]
    zero = jnp.zeros((16, 128), f32)
    for c in range(3):
        pack_ref[15 + c, 48:64, :] = zero
    s = jnp.where(lanes_low(top.shape), top, bot)
    return s + swap_halves(s)


def leaf_rows(pack_ref, leaf):
    row = lax.broadcasted_iota(jnp.int32, (8, PTS), 0)
    out = jnp.zeros((8, PTS), f32)
    for c in range(3):
        line = jnp.concatenate(
            [pack_ref[15 + c, 2 * leaf:2 * leaf + 1, :], pack_ref[15 + c, 2 * leaf + 1:2 * leaf + 2, :]], axis=1
        )
        out = jnp.where(row == c, line, out)
    return out


def pieces(a):
    h = a.astype(bf16).astype(f32)
    r = a - h
    m = r.astype(bf16).astype(f32)
    return h, m, r - m


def identity():
    return jnp.where(
        lax.broadcasted_iota(jnp.int32, (PTS, PTS), 0) == lax.broadcasted_iota(jnp.int32, (PTS, PTS), 1), 1.0, 0.0
    ).astype(bf16)


def prepare(pack_ref, x_ref, leaf, at, eye, centres, feats, xs):
    row = lax.broadcasted_iota(jnp.int32, (8, PTS), 0)
    source = leaf_rows(pack_ref, leaf)
    centre = jnp.broadcast_to(jnp.sum(source, axis=1, keepdims=True) * (1.0 / PTS), (8, PTS))
    centres[at] = centre
    d = source - centre
    sq = jnp.sum(d * d, axis=0, keepdims=True) + smooth_sq
    h, m, l = pieces(jnp.where(row < 3, -2.0 * d, jnp.where(row == 3, 1.0, jnp.where(row == 4, sq, 0.0))))
    rows = jnp.concatenate([h, m, h, l, m, h, jnp.zeros((80, PTS), f32)], axis=0).astype(bf16)
    feats[at] = dot(eye, rows, NT).astype(bf16)
    xh, xl = split(x_ref[:, leaf * PTS:leaf * PTS + PTS] * inv_four_pi)
    xs[at] = jnp.concatenate([xh, xl], axis=0)


def pairs(ls, js, targets, centres, feats, xs, acc):
    unit = jnp.where(lax.broadcasted_iota(jnp.int32, (8, PTS), 0) == 4, 1.0, 0.0)
    row = lax.broadcasted_iota(jnp.int32, (8, PTS), 0)
    dist = []
    for l, j in zip(ls, js):
        d = targets[l] - centres[j]
        sq = jnp.sum(d * d, axis=0, keepdims=True)
        h, m, low = pieces(jnp.where(row == 3, sq, d + unit))
        rows = jnp.concatenate([h, h, m, h, m, low], axis=0).astype(bf16)
        dist.append(dot(feats[j][:, :48], rows))
    for l, j, d2 in zip(ls, js, dist):
        kh, kl = split(lax.rsqrt(d2))
        x = xs[j]
        r = dot(x, kh) + dot(x, kl)
        acc[l] += r[:64] + r[64:]


def place_tile(tile, low_ref, high_ref, at):
    other = swap_halves(tile)
    low = lanes_low(tile.shape)
    for i, (here, there) in enumerate(((tile, other), (other, tile))):
        h, l = split(jnp.where(low, here, 0.0))
        low_ref[at + i] = jnp.concatenate([h, l], axis=0)
        h, l = split(jnp.where(low, 0.0, there))
        high_ref[at + i] = jnp.concatenate([h, l], axis=0)


def coupled(sources, weights, low_ref, high_ref):
    lhs = jnp.concatenate(
        [
            jnp.concatenate([low_ref[row[f]] + high_ref[row[f + 1]] for f in range(0, len(row), 2)], axis=1)
            for row in sources
        ],
        axis=0,
    )
    out = dot(lhs, wide_split(jnp.concatenate(weights, axis=0)))
    s = out[:, :128] + out[:, 128:]
    even, odd = s[0:64] + s[64:128], s[128:192] + s[192:256]
    return jnp.where(lanes_low(even.shape), even, odd)


def top_coupled(picks, c2_ref):
    tiles = []
    for f in range(0, FAR2, 2):
        a = jnp.concatenate([picks[f], swap_halves(picks[f])], axis=0)
        b = jnp.concatenate([swap_halves(picks[f + 1]), picks[f + 1]], axis=0)
        tiles.append(jnp.where(lanes_low(a.shape), a, b))
    th, tl = split(jnp.concatenate(tiles, axis=1))
    w = jnp.concatenate([c2_ref[f] for f in range(FAR2)], axis=0)
    wh, wl = split(jnp.concatenate([w, w], axis=1))
    y2 = dot(th, wh) + dot(tl, wh) + dot(th, wl)
    return jnp.where(lanes_low((32, 128)), y2[:32], y2[32:])


def main_kernel(
    list_ref, far0_ref, far1_ref, far2_ref, coords_hbm, x_hbm, basis_hbm, t1_hbm, t2_hbm, c0_hbm, c1_hbm, c2_hbm,
    acc_out, pack_out, p2_ref, x2_ref, centres_out, feats_out, xs_out,
    coords, x, x1, basis, t1, t2, c0, c1, c2, pack, p1, p2, acc, targets, centres, feats, xs,
    part, parts, y2_part, y2_parts, y1, q_low, q_high, m_low, m_high,
    load_sem, part_send, part_recv, y2_send, y2_recv, pack_send, pack_recv, e_send, e_recv, n_send, n_recv, out_sem,
):
    group = lax.axis_index("grp")
    lane = lax.axis_index("lane")
    place = group * LANES + lane
    even = lax.rem(lane, 2) == 0
    partner = (group, lane + 1 - 2 * lax.rem(lane, 2))
    beyond = lax.rem(place + jnp.where(even, DEVS - 1, 1), DEVS)
    beyond = (beyond // LANES, lax.rem(beyond, LANES))

    barrier = pltpu.get_barrier_semaphore()
    for d in range(1, LANES):
        pl.semaphore_signal(barrier, inc=1, device_id=(group, lax.rem(lane + d, LANES)), device_id_type=MESH)
    for d in range(1, GROUPS):
        pl.semaphore_signal(barrier, inc=1, device_id=(lax.rem(group + d, GROUPS), lane), device_id_type=MESH)
    pl.semaphore_signal(barrier, inc=1, device_id=beyond, device_id_type=MESH)

    loads = [
        pltpu.make_async_copy(src, dst, load_sem.at[i])
        for i, (src, dst) in enumerate(
            [(x_hbm.at[:, c * 1536:c * 1536 + 1536], x.at[:, c * 1536:c * 1536 + 1536]) for c in range(4)]
            + [(basis_hbm.at[r * 64:r * 64 + 64], basis.at[r * 64:r * 64 + 64]) for r in range(4)]
            + [(t1_hbm, t1), (t2_hbm, t2), (coords_hbm, coords)]
            + [(c0_hbm.at[r * 2:r * 2 + 2], c0.at[r * 2:r * 2 + 2]) for r in range(4)]
            + [(c1_hbm, c1), (c2_hbm, c2)]
        )
    ]
    for c in loads:
        c.start()
    for c in loads[:11]:
        c.wait()
    top = upward(coords, x, basis, t1, t2, pack)
    part[...] = jnp.where(lanes_low((32, 128)), top[:32], top[32:])
    pl.semaphore_wait(barrier, LANES + GROUPS - 1)

    def part_copy(d):
        peer = lax.rem(group + d, GROUPS)
        return (
            pltpu.make_async_remote_copy(
                part, parts.at[group], part_send.at[d], part_recv.at[group], (peer, lane), MESH
            ),
            pltpu.make_async_remote_copy(
                part, parts.at[peer], part_send.at[d], part_recv.at[peer], (peer, lane), MESH
            ),
        )

    def y2_copy(d):
        peer = lax.rem(lane + d, LANES)
        return (
            pltpu.make_async_remote_copy(
                y2_part, y2_parts.at[lane], y2_send.at[d], y2_recv.at[lane], (group, peer), MESH
            ),
            pltpu.make_async_remote_copy(
                y2_part, y2_parts.at[peer], y2_send.at[d], y2_recv.at[peer], (group, peer), MESH
            ),
        )

    def chunk(i, src, dst, send, recv, device):
        at = (slice(None), pl.ds(pl.multiple_of(i * CHUNK, CHUNK), CHUNK))
        return pltpu.make_async_remote_copy(src.at[at], dst.at[at], send.at[i], recv.at[i], device, MESH)

    def near_chunks(i):
        return chunk(i, x, x2_ref, n_send, n_recv, beyond), chunk(i, x, x1, e_send, e_recv, partner)

    for d in range(1, GROUPS):
        part_copy(d)[0].start()
    packs = [
        pltpu.make_async_remote_copy(pack, p2, pack_send.at[0], pack_recv.at[0], beyond, MESH),
        pltpu.make_async_remote_copy(pack, p1, pack_send.at[1], pack_recv.at[1], partner, MESH),
    ]
    for c in packs:
        c.start()
    for c in near_chunks(0):
        c.start()

    eye = identity()
    for leaf in range(LEAF):
        targets[leaf] = leaf_rows(pack, leaf)
        prepare(pack, x, leaf, leaf, eye, centres, feats, xs)
        acc[leaf] = jnp.zeros((64, PTS), f32)
    centres[2 * LEAF] = jnp.zeros((8, PTS), f32)
    feats[2 * LEAF] = feats[0]
    xs[2 * LEAF] = jnp.zeros((128, PTS), bf16)

    def leaves(i):
        ls = [2 * i + u for u in range(2) for s in range(SLOTS)]
        js = [list_ref[s, 2 * i + u] for u in range(2) for s in range(SLOTS)]
        pairs(ls, [jnp.where(j == LEAF, 2 * LEAF, j) for j in js], targets, centres, feats, xs, acc)

    def step(i, _):
        for c in near_chunks(i + 1):
            c.start()
        leaves(i)
        return 0

    lax.fori_loop(0, 4, step, 0)

    for c in loads[11:]:
        c.wait()
    for d in range(1, GROUPS):
        part_copy(d)[1].wait_recv()
    parts[group] = part[...]
    mine = top_coupled([parts[far2_ref[f, group]] for f in range(FAR2)], c2)
    y2_part[...] = mine
    y2_parts[lane] = mine
    for d in range(1, LANES):
        y2_copy(d)[0].start()

    lax.fori_loop(4, LEAF // 2 - 1, step, 0)
    leaves(LEAF // 2 - 1)

    for c in packs:
        c.wait()
    for b, p in enumerate((pack, p1, p2)):
        for t in range(LEAF // 2):
            place_tile(p[t], q_low, q_high, LEAF * b + 2 * t)
        for t in range(MID // 2):
            place_tile(p[LEAF // 2 + t], m_low, m_high, MID * b + 2 * t)
    for d in range(1, LANES):
        y2_copy(d)[1].wait_recv()
    y2 = y2_parts[0]
    for r in range(1, LANES):
        y2 = y2 + y2_parts[r]
    other = swap_halves(y2)
    low = lanes_low(y2.shape)
    y2 = jnp.concatenate([jnp.where(low, y2, other), jnp.where(low, other, y2)], axis=0)

    for t in range(MID // 2):
        at = slice(t * 128, t * 128 + 128)
        y = coupled(
            [[source_of(far1_ref[f, 2 * t + i], place, MID) for f in range(FAR1)] for i in range(2)],
            [c1[f, :, at] for f in range(FAR1)], m_low, m_high,
        )
        w = t2[:, at]
        one, two = transposed(*halves(y2), jnp.concatenate([w, w], axis=0))
        y = y + jnp.where(lanes_low(y.shape), one, two)
        other = swap_halves(y)
        low = lanes_low(y.shape)
        y1[2 * t] = jnp.where(low, y, other)
        y1[2 * t + 1] = jnp.where(low, other, y)

    def down(m, _):
        for u in range(2):
            t = 2 * m + u
            at = pl.ds(pl.multiple_of(t * 128, 128), 128)
            y = coupled(
                [[source_of(far0_ref[f, 2 * t + i], place, LEAF) for f in range(FAR0)] for i in range(2)],
                [c0[f, :, at] for f in range(FAR0)], q_low, q_high,
            )
            w = t1[:, at]
            one, two = transposed(*halves(y1[m]), jnp.concatenate([w, w], axis=0))
            y = y + jnp.where(lanes_low(y.shape), one, two)
            one, two = transposed(*halves(y), basis[:, at])
            acc[2 * t] += one
            acc[2 * t + 1] += two
        return 0

    lax.fori_loop(0, MID, down, 0)

    def arrived(i, _):
        chunk(i, x, x1, e_send, e_recv, partner).wait()
        return 0

    lax.fori_loop(0, LEAF // 2, arrived, 0)
    for leaf in range(LEAF):
        prepare(p1, x1, leaf, LEAF + leaf, eye, centres, feats, xs)
    outs = [
        pltpu.make_async_copy(src, dst, out_sem.at[i])
        for i, (src, dst) in enumerate(
            [
                (acc, acc_out), (pack, pack_out), (p2, p2_ref), (centres.at[0:48], centres_out),
                (feats.at[0:24], feats_out.at[0:24]), (feats.at[24:48], feats_out.at[24:48]),
                (xs.at[0:24], xs_out.at[0:24]), (xs.at[24:48], xs_out.at[24:48]),
            ]
        )
    ]
    for c in outs:
        c.start()
    for d in range(1, GROUPS):
        part_copy(d)[0].wait_send()
    for d in range(1, LANES):
        y2_copy(d)[0].wait_send()

    def sent(i, _):
        chunk(i, x, x2_ref, n_send, n_recv, beyond).wait()
        return 0

    lax.fori_loop(0, LEAF // 2, sent, 0)
    for c in outs:
        c.wait()


def rest_kernel(
    list_ref, own_hbm, p2_hbm, x2_hbm, acc_hbm, centres_hbm, feats_hbm, xs_hbm, out_ref,
    own, p2, targets, centres, feats, xs, acc, x, sem,
):
    moves = [
        pltpu.make_async_copy(src, dst, sem.at[i])
        for i, (src, dst) in enumerate(
            [(own_hbm, own), (p2_hbm, p2)]
            + [(x2_hbm.at[:, c * 1536:c * 1536 + 1536], x.at[:, c * 1536:c * 1536 + 1536]) for c in range(4)]
            + [
                (acc_hbm, acc.at[0:24]), (centres_hbm, centres.at[0:48]),
                (feats_hbm.at[0:24], feats.at[0:24]), (feats_hbm.at[24:48], feats.at[24:48]),
                (xs_hbm.at[0:24], xs.at[0:24]), (xs_hbm.at[24:48], xs.at[24:48]),
            ]
        )
    ]
    for c in moves:
        c.start()
    targets[LEAF] = jnp.zeros((8, PTS), f32)
    acc[LEAF] = jnp.zeros((64, PTS), f32)
    eye = identity()
    for c in moves[:6]:
        c.wait()
    for leaf in range(LEAF):
        targets[leaf] = leaf_rows(own, leaf)
        prepare(p2, x, leaf, 2 * LEAF + leaf, eye, centres, feats, xs)
    for c in moves[6:]:
        c.wait()

    @pl.loop(0, (list_ref[COUNT_ROW, 0] + (UNROLL - 1)) // UNROLL)
    def _(i):
        words = [list_ref[REST_ROW, i * UNROLL + u] for u in range(UNROLL)]
        pairs(
            [lax.shift_right_logical(w, 7) for w in words], [w & 127 for w in words], targets, centres, feats, xs, acc
        )

    for leaf in range(LEAF):
        out_ref[:, leaf * PTS:leaf * PTS + PTS] = acc[leaf]


VM = pl.BlockSpec(memory_space=pltpu.VMEM)
SM = pl.BlockSpec(memory_space=pltpu.SMEM)
ANY = pl.BlockSpec(memory_space=pl.ANY)
DMA = pltpu.SemaphoreType.DMA


def params(mib, **more):
    return pltpu.CompilerParams(vmem_limit_bytes=mib << 20, **more)


def cost(size):
    return pl.CostEstimate(flops=size, bytes_accessed=1000, transcendentals=0)


def shape(*dims, dtype=f32):
    return jax.ShapeDtypeStruct(dims, dtype)


def local(
    coords, charges, basis, transfer1, transfer2, coupling0, coupling1, coupling2, near_list, near_count, far0_list,
    far1_list, far2_list,
):
    lists = pl.pallas_call(
        list_kernel, out_shape=shape(16, PTS, dtype=jnp.int32), in_specs=[VM, VM], out_specs=VM,
        compiler_params=params(56), cost_estimate=cost(1000), name="lists",
    )(near_list.T, near_count.reshape(1, LEAF))
    wide = LEAF * PTS
    acc, pack, p2, x2, centres, feats, xs = pl.pallas_call(
        main_kernel,
        out_shape=(
            shape(LEAF, 64, PTS), shape(18, 64, 128), shape(18, 64, 128), shape(64, wide), shape(2 * LEAF, 8, PTS),
            shape(2 * LEAF, PTS, 128, dtype=bf16), shape(2 * LEAF, 128, PTS, dtype=bf16),
        ),
        in_specs=[SM] * 4 + [ANY] * 8,
        out_specs=(ANY,) * 7,
        scratch_shapes=[
            pltpu.VMEM((3, wide), f32), pltpu.VMEM((64, wide), f32), pltpu.VMEM((64, wide), f32),
            pltpu.VMEM((PTS, LEAF * RANK), f32), pltpu.VMEM((RANK, LEAF * RANK), f32),
            pltpu.VMEM((RANK, MID * RANK), f32), pltpu.VMEM((FAR0, RANK, LEAF * RANK), f32),
            pltpu.VMEM((FAR1, RANK, MID * RANK), f32), pltpu.VMEM((FAR2, RANK, RANK), f32),
            pltpu.VMEM((18, 64, 128), f32), pltpu.VMEM((18, 64, 128), f32), pltpu.VMEM((18, 64, 128), f32),
            pltpu.VMEM((LEAF, 64, PTS), f32), pltpu.VMEM((LEAF, 8, PTS), f32),
            pltpu.VMEM((2 * LEAF + 1, 8, PTS), f32), pltpu.VMEM((2 * LEAF + 1, PTS, 128), bf16),
            pltpu.VMEM((2 * LEAF + 1, 128, PTS), bf16),
            pltpu.VMEM((32, 128), f32), pltpu.VMEM((GROUPS, 32, 128), f32), pltpu.VMEM((32, 128), f32),
            pltpu.VMEM((LANES, 32, 128), f32), pltpu.VMEM((MID, 64, 128), f32),
            pltpu.VMEM((3 * LEAF, 128, 128), bf16), pltpu.VMEM((3 * LEAF, 128, 128), bf16),
            pltpu.VMEM((3 * MID, 128, 128), bf16), pltpu.VMEM((3 * MID, 128, 128), bf16),
            DMA((17,)), DMA((GROUPS,)), DMA((GROUPS,)), DMA((LANES,)), DMA((LANES,)), DMA((2,)), DMA((2,)),
            DMA((LEAF // 2,)), DMA((LEAF // 2,)), DMA((LEAF // 2,)), DMA((LEAF // 2,)), DMA((8,)),
        ],
        compiler_params=params(56, collective_id=0, has_side_effects=True),
        cost_estimate=cost(1000),
        name="main",
    )(
        lists, far0_list.T, far1_list.T, far2_list.T, coords, charges, basis, transfer1, transfer2, coupling0,
        coupling1, coupling2,
    )
    return pl.pallas_call(
        rest_kernel,
        out_shape=shape(64, wide),
        in_specs=[SM] + [ANY] * 7,
        out_specs=VM,
        scratch_shapes=[
            pltpu.VMEM((18, 64, 128), f32), pltpu.VMEM((18, 64, 128), f32), pltpu.VMEM((LEAF + 1, 8, PTS), f32),
            pltpu.VMEM((3 * LEAF, 8, PTS), f32), pltpu.VMEM((3 * LEAF, PTS, 128), bf16),
            pltpu.VMEM((3 * LEAF, 128, PTS), bf16), pltpu.VMEM((LEAF + 1, 64, PTS), f32), pltpu.VMEM((64, wide), f32),
            DMA((12,)),
        ],
        compiler_params=params(56),
        cost_estimate=cost(1000),
        name="rest",
    )(lists, pack, p2, x2, acc, centres, feats, xs)


def solution(mesh):
    placed = (
        P(None, AXES),
        P(None, AXES),
        P(None, AXES),
        P(None, AXES),
        P(None, AXES),
        P(None, None, AXES),
        P(None, None, AXES),
        P(None, None, "grp"),
        P(AXES, None),
        P(AXES),
        P(AXES, None),
        P(AXES, None),
        P(),
    )
    return jax.shard_map(local, mesh=mesh, in_specs=placed, out_specs=P(None, AXES), check_vma=False)
```

```python
import math

import jax
import jax.numpy as jnp
from jax import lax
from jax.experimental import pallas as pl
from jax.experimental.pallas import tpu as pltpu
from jax.sharding import PartitionSpec as P

AXES = ("grp", "lane")
LANES = 8
DEVS = 128
LEAF = 24
MID = 6
PTS = 256
RANK = 64
NEAR = 9
FAR0 = 8
FAR1 = 4
FAR2 = 4
UNROLL = 24
SLOTS = 5
REST_ROW = 8
COUNT_ROW = 9
AHEAD = 2048
STEP = 4
GROUPS = 16
MESH = pl.DeviceIdType.MESH
inv_four_pi = 1.0 / (4.0 * math.pi)
smooth_sq = 5e-05
bf16 = jnp.bfloat16
f32 = jnp.float32
NT = (((1,), (1,)), ((), ()))


def dot(a, b, dims=(((1,), (0,)), ((), ()))):
    return lax.dot_general(a, b, dims, preferred_element_type=f32)


def split(a):
    high = a.astype(bf16)
    return high, (a - high.astype(f32)).astype(bf16)


def lanes_low(shape):
    return lax.broadcasted_iota(jnp.int32, shape, len(shape) - 1) < RANK


def swap_halves(a):
    return pltpu.roll(a, RANK, 1)


def halves(tile):
    low = lanes_low(tile.shape)
    return jnp.where(low, tile, 0.0), jnp.where(low, 0.0, tile)


def place_of():
    return lax.axis_index("grp") * LANES + lax.axis_index("lane")


def source_of(entry, place, width):
    even = lax.rem(place, 2) == 0
    rel = entry - place * width
    rel = jnp.where(rel < -width, rel + DEVS * width, jnp.where(rel >= 2 * width, rel - DEVS * width, rel))
    low_off = jnp.where(even, 3 * width, 2 * width)
    high_off = jnp.where(even, 0, width)
    source = rel + jnp.where(rel < 0, low_off, jnp.where(rel >= width, high_off, 0))
    return jnp.minimum(jnp.maximum(source, 0), 3 * width - 1)


def stacked_split(rows_a, rows_b):
    ah, al = split(rows_a)
    bh, bl = split(rows_b)
    return jnp.concatenate([ah, bh, al, bl], axis=0)


def wide_split(a):
    h, l = split(a)
    return jnp.concatenate([h, l], axis=1)


def fold(out):
    s = out[:, :128] + out[:, 128:]
    return s[0:64] + s[128:192], s[64:128] + s[192:256]


def transposed(rows_a, rows_b, weights):
    lhs = stacked_split(rows_a, rows_b)
    wh, wl = split(weights)
    r = dot(lhs, wh, NT)
    r2 = dot(lhs[:128], wl, NT)
    return r[0:64] + r[128:192] + r2[0:64], r[64:128] + r[192:256] + r2[64:128]


def list_kernel(near_ref, count_ref, out_ref):
    place = place_of()
    source = source_of(near_ref[...], place, LEAF)
    count = count_ref[...]
    leaf = lax.broadcasted_iota(jnp.int32, (1, LEAF), 1)
    own_at = jnp.zeros((1, LEAF), jnp.int32)
    rest_at = jnp.zeros((1, LEAF), jnp.int32)
    own = [jnp.full((1, LEAF), LEAF, jnp.int32) for _ in range(SLOTS - 1)]
    places = []
    for k in range(1, NEAR):
        src = source[k:k + 1]
        live = count > k
        here = jnp.logical_and(jnp.logical_and(src < LEAF, live), own_at < SLOTS - 1)
        for s in range(SLOTS - 1):
            own[s] = jnp.where(jnp.logical_and(here, own_at == s), src, own[s])
        own_at = own_at + jnp.where(here, 1, 0)
        rest = jnp.logical_and(live, jnp.logical_not(here))
        places.append((rest, rest_at))
        rest_at = rest_at + jnp.where(rest, 1, 0)
    row = lax.broadcasted_iota(jnp.int32, (LEAF, LEAF), 0)
    col = lax.broadcasted_iota(jnp.int32, (LEAF, LEAF), 1)
    before = jnp.where(row < col, 1.0, 0.0).astype(bf16)
    counts = jnp.broadcast_to(rest_at.astype(f32), (16, LEAF)).astype(bf16)
    base = dot(counts, before)[0:1]
    at = [jnp.where(rest, base + pos.astype(f32), -1.0) for rest, pos in places]
    values = jnp.concatenate(at + [source[k:k + 1].astype(f32) for k in range(1, NEAR)], axis=0).astype(bf16)
    columns = dot(jnp.where(row == col, 1.0, 0.0).astype(bf16), values, NT)
    lanes = lax.broadcasted_iota(jnp.int32, (LEAF, PTS), 1).astype(f32)
    word = lax.broadcasted_iota(jnp.int32, (LEAF, 1), 0).astype(f32) * 128.0
    flat = jnp.zeros((LEAF, PTS), f32)
    for k in range(NEAR - 1):
        flat = flat + jnp.where(columns[:, k:k + 1] == lanes, word + columns[:, NEAR - 1 + k:NEAR + k], 0.0)
    flat = jnp.sum(flat, axis=0, keepdims=True)
    total = jnp.sum(rest_at.astype(f32), axis=1, keepdims=True)
    flat = jnp.where(lanes[0:1] < total, flat, LEAF * 128.0)
    out_ref[...] = jnp.zeros((16, PTS), jnp.int32)
    out_ref[0:1, 0:LEAF] = leaf
    for s in range(SLOTS - 1):
        out_ref[s + 1:s + 2, 0:LEAF] = own[s]
    out_ref[REST_ROW:REST_ROW + 1, :] = flat.astype(jnp.int32)
    out_ref[COUNT_ROW:COUNT_ROW + 1, :] = jnp.broadcast_to(total, (1, PTS)).astype(jnp.int32)


def upward(coords_ref, x_ref, basis_ref, t1_ref, t2_ref, pack_ref):
    tiles = []
    for t in range(LEAF // 2):
        xa = x_ref[:, t * 512:t * 512 + 256]
        xb = x_ref[:, t * 512 + 256:t * 512 + 512]
        ra, rb = fold(dot(stacked_split(xa, xb), wide_split(basis_ref[:, t * 128:t * 128 + 128])))
        q = jnp.where(lanes_low(ra.shape), ra, rb)
        pack_ref[t] = q
        tiles.append(q)
    mids = []
    parts = []
    for m in range(MID):
        a0, b0 = halves(tiles[2 * m])
        a1, b1 = halves(tiles[2 * m + 1])
        e0 = t1_ref[:, m * 256:m * 256 + 128]
        e1 = t1_ref[:, m * 256 + 128:m * 256 + 256]
        lhs = stacked_split(jnp.concatenate([a0, a1], axis=1), jnp.concatenate([b0, b1], axis=1))
        parts.append(fold(dot(lhs, wide_split(jnp.concatenate([e0, e0, e1, e1], axis=0)))))
    for t in range(MID // 2):
        (top0, bot0), (top1, bot1) = parts[2 * t], parts[2 * t + 1]
        low = lanes_low(top0.shape)
        mid = jnp.where(low, top0, bot1) + swap_halves(jnp.where(low, top1, bot0))
        pack_ref[LEAF // 2 + t] = mid
        mids.append(mid)
    both = [halves(m) for m in mids]
    weights = [t2_ref[:, t * 128:t * 128 + 128] for t in range(MID // 2)]
    lhs = stacked_split(
        jnp.concatenate([b[0] for b in both], axis=1), jnp.concatenate([b[1] for b in both], axis=1)
    )
    top, bot = fold(dot(lhs, wide_split(jnp.concatenate([w for w in weights for _ in range(2)], axis=0))))
    for i in range(2 * LEAF):
        for c in range(3):
            pack_ref[15 + c, i:i + 1, :] = coords_ref[c:c + 1, i * 128:i * 128 + 128]
    zero = jnp.zeros((16, 128), f32)
    for c in range(3):
        pack_ref[15 + c, 48:64, :] = zero
    s = jnp.where(lanes_low(top.shape), top, bot)
    return s + swap_halves(s)


def leaf_rows(pack_ref, leaf):
    row = lax.broadcasted_iota(jnp.int32, (8, PTS), 0)
    out = jnp.zeros((8, PTS), f32)
    for c in range(3):
        line = jnp.concatenate(
            [pack_ref[15 + c, 2 * leaf:2 * leaf + 1, :], pack_ref[15 + c, 2 * leaf + 1:2 * leaf + 2, :]], axis=1
        )
        out = jnp.where(row == c, line, out)
    return out


def pieces(a):
    h = a.astype(bf16).astype(f32)
    r = a - h
    m = r.astype(bf16).astype(f32)
    return h, m, r - m


def identity():
    return jnp.where(
        lax.broadcasted_iota(jnp.int32, (PTS, PTS), 0) == lax.broadcasted_iota(jnp.int32, (PTS, PTS), 1), 1.0, 0.0
    ).astype(bf16)


def prepare(pack_ref, x_ref, leaf, at, eye, centres, feats, xs):
    row = lax.broadcasted_iota(jnp.int32, (8, PTS), 0)
    source = leaf_rows(pack_ref, leaf)
    centre = jnp.broadcast_to(jnp.sum(source, axis=1, keepdims=True) * (1.0 / PTS), (8, PTS))
    centres[at] = centre
    d = source - centre
    sq = jnp.sum(d * d, axis=0, keepdims=True) + smooth_sq
    h, m, l = pieces(jnp.where(row < 3, -2.0 * d, jnp.where(row == 3, 1.0, jnp.where(row == 4, sq, 0.0))))
    rows = jnp.concatenate([h, m, h, l, m, h, jnp.zeros((80, PTS), f32)], axis=0).astype(bf16)
    feats[at] = dot(eye, rows, NT).astype(bf16)
    xh, xl = split(x_ref[:, leaf * PTS:leaf * PTS + PTS] * inv_four_pi)
    xs[at] = jnp.concatenate([xh, xl], axis=0)


def pairs(ls, js, targets, centres, feats, xs, acc):
    unit = jnp.where(lax.broadcasted_iota(jnp.int32, (8, PTS), 0) == 4, 1.0, 0.0)
    row = lax.broadcasted_iota(jnp.int32, (8, PTS), 0)
    dist = []
    for l, j in zip(ls, js):
        d = targets[l] - centres[j]
        sq = jnp.sum(d * d, axis=0, keepdims=True)
        h, m, low = pieces(jnp.where(row == 3, sq, d + unit))
        rows = jnp.concatenate([h, h, m, h, m, low], axis=0).astype(bf16)
        dist.append(dot(feats[j][:, :48], rows))
    for l, j, d2 in zip(ls, js, dist):
        kh, kl = split(lax.rsqrt(d2))
        x = xs[j]
        r = dot(x, kh) + dot(x, kl)
        acc[l] += r[:64] + r[64:]


def place_tile(tile, low_ref, high_ref, at):
    other = swap_halves(tile)
    low = lanes_low(tile.shape)
    for i, (here, there) in enumerate(((tile, other), (other, tile))):
        h, l = split(jnp.where(low, here, 0.0))
        low_ref[at + i] = jnp.concatenate([h, l], axis=0)
        h, l = split(jnp.where(low, 0.0, there))
        high_ref[at + i] = jnp.concatenate([h, l], axis=0)


def coupled(sources, weights, low_ref, high_ref):
    lhs = jnp.concatenate(
        [
            jnp.concatenate([low_ref[row[f]] + high_ref[row[f + 1]] for f in range(0, len(row), 2)], axis=1)
            for row in sources
        ],
        axis=0,
    )
    out = dot(lhs, wide_split(jnp.concatenate(weights, axis=0)))
    s = out[:, :128] + out[:, 128:]
    even, odd = s[0:64] + s[64:128], s[128:192] + s[192:256]
    return jnp.where(lanes_low(even.shape), even, odd)


def top_coupled(picks, c2_ref):
    tiles = []
    for f in range(0, FAR2, 2):
        a = jnp.concatenate([picks[f], swap_halves(picks[f])], axis=0)
        b = jnp.concatenate([swap_halves(picks[f + 1]), picks[f + 1]], axis=0)
        tiles.append(jnp.where(lanes_low(a.shape), a, b))
    th, tl = split(jnp.concatenate(tiles, axis=1))
    w = jnp.concatenate([c2_ref[f] for f in range(FAR2)], axis=0)
    wh, wl = split(jnp.concatenate([w, w], axis=1))
    y2 = dot(th, wh) + dot(tl, wh) + dot(th, wl)
    return jnp.where(lanes_low((32, 128)), y2[:32], y2[32:])


def main_kernel(
    list_ref, far0_ref, far1_ref, far2_ref, coords_hbm, x_hbm, basis_hbm, t1_hbm, t2_hbm, c0_hbm, c1_hbm, c2_hbm,
    acc_out, pack_out, p2_ref, x2_ref, centres_out, feats_out, xs_out,
    coords, x, x1, basis, t1, t2, c0, c1, c2, pack, p1, p2, acc, targets, centres, feats, xs,
    part, parts, y2_part, y2_parts, y1, q_low, q_high, m_low, m_high,
    load_sem, part_send, part_recv, y2_send, y2_recv, swap_send, swap_recv, out_sem,
):
    group = lax.axis_index("grp")
    lane = lax.axis_index("lane")
    place = group * LANES + lane
    even = lax.rem(lane, 2) == 0
    partner = (group, lane + 1 - 2 * lax.rem(lane, 2))
    beyond = lax.rem(place + jnp.where(even, DEVS - 1, 1), DEVS)
    beyond = (beyond // LANES, lax.rem(beyond, LANES))

    barrier = pltpu.get_barrier_semaphore()
    for d in range(1, LANES):
        pl.semaphore_signal(barrier, inc=1, device_id=(group, lax.rem(lane + d, LANES)), device_id_type=MESH)
    for d in range(1, GROUPS):
        pl.semaphore_signal(barrier, inc=1, device_id=(lax.rem(group + d, GROUPS), lane), device_id_type=MESH)
    pl.semaphore_signal(barrier, inc=1, device_id=beyond, device_id_type=MESH)

    loads = [
        pltpu.make_async_copy(src, dst, load_sem.at[i])
        for i, (src, dst) in enumerate(
            [(x_hbm.at[:, c * 1536:c * 1536 + 1536], x.at[:, c * 1536:c * 1536 + 1536]) for c in range(4)]
            + [(basis_hbm.at[r * 64:r * 64 + 64], basis.at[r * 64:r * 64 + 64]) for r in range(4)]
            + [(t1_hbm, t1), (t2_hbm, t2), (coords_hbm, coords)]
            + [(c0_hbm.at[r * 2:r * 2 + 2], c0.at[r * 2:r * 2 + 2]) for r in range(4)]
            + [(c1_hbm, c1), (c2_hbm, c2)]
        )
    ]
    for c in loads:
        c.start()
    for c in loads[:11]:
        c.wait()
    top = upward(coords, x, basis, t1, t2, pack)
    part[...] = jnp.where(lanes_low((32, 128)), top[:32], top[32:])
    pl.semaphore_wait(barrier, LANES + GROUPS - 1)

    def part_copy(d):
        peer = lax.rem(group + d, GROUPS)
        return (
            pltpu.make_async_remote_copy(
                part, parts.at[group], part_send.at[d], part_recv.at[group], (peer, lane), MESH
            ),
            pltpu.make_async_remote_copy(
                part, parts.at[peer], part_send.at[d], part_recv.at[peer], (peer, lane), MESH
            ),
        )

    def y2_copy(d):
        peer = lax.rem(lane + d, LANES)
        return (
            pltpu.make_async_remote_copy(
                y2_part, y2_parts.at[lane], y2_send.at[d], y2_recv.at[lane], (group, peer), MESH
            ),
            pltpu.make_async_remote_copy(
                y2_part, y2_parts.at[peer], y2_send.at[d], y2_recv.at[peer], (group, peer), MESH
            ),
        )

    def swap(src, dst, i, device):
        return pltpu.make_async_remote_copy(src, dst, swap_send.at[i], swap_recv.at[i], device, MESH)

    swaps = [
        swap(x, x1, 0, partner),
        swap(x.at[:, 0:AHEAD], x2_ref.at[:, 0:AHEAD], 1, beyond),
        swap(pack, p1, 2, partner),
        swap(pack, p2, 3, beyond),
        swap(x.at[:, AHEAD:], x2_ref.at[:, AHEAD:], 4, beyond),
    ]
    for d in range(1, GROUPS):
        part_copy(d)[0].start()
    swaps[0].start()
    swaps[1].start()

    eye = identity()
    for leaf in range(LEAF):
        targets[leaf] = leaf_rows(pack, leaf)
        prepare(pack, x, leaf, leaf, eye, centres, feats, xs)
        acc[leaf] = jnp.zeros((64, PTS), f32)
    centres[2 * LEAF] = jnp.zeros((8, PTS), f32)
    feats[2 * LEAF] = feats[0]
    xs[2 * LEAF] = jnp.zeros((128, PTS), bf16)

    def leaves(i, _):
        at = [STEP * i + u for u in range(STEP) for s in range(SLOTS)]
        js = [list_ref[s, STEP * i + u] for u in range(STEP) for s in range(SLOTS)]
        pairs(at, [jnp.where(j == LEAF, 2 * LEAF, j) for j in js], targets, centres, feats, xs, acc)
        return 0

    lax.fori_loop(0, 2, leaves, 0)

    for c in loads[11:]:
        c.wait()
    for d in range(1, GROUPS):
        part_copy(d)[1].wait_recv()
    parts[group] = part[...]
    mine = top_coupled([parts[far2_ref[f, group]] for f in range(FAR2)], c2)
    y2_part[...] = mine
    y2_parts[lane] = mine
    for d in range(1, LANES):
        y2_copy(d)[0].start()

    for c in swaps[2:]:
        c.start()

    lax.fori_loop(2, LEAF // STEP, leaves, 0)

    for c in swaps[2:4]:
        c.wait()
    for b, p in enumerate((pack, p1, p2)):
        for t in range(LEAF // 2):
            place_tile(p[t], q_low, q_high, LEAF * b + 2 * t)
        for t in range(MID // 2):
            place_tile(p[LEAF // 2 + t], m_low, m_high, MID * b + 2 * t)
    for d in range(1, LANES):
        y2_copy(d)[1].wait_recv()
    y2 = y2_parts[0]
    for r in range(1, LANES):
        y2 = y2 + y2_parts[r]
    other = swap_halves(y2)
    low = lanes_low(y2.shape)
    y2 = jnp.concatenate([jnp.where(low, y2, other), jnp.where(low, other, y2)], axis=0)

    for t in range(MID // 2):
        at = slice(t * 128, t * 128 + 128)
        y = coupled(
            [[source_of(far1_ref[f, 2 * t + i], place, MID) for f in range(FAR1)] for i in range(2)],
            [c1[f, :, at] for f in range(FAR1)], m_low, m_high,
        )
        w = t2[:, at]
        one, two = transposed(*halves(y2), jnp.concatenate([w, w], axis=0))
        y = y + jnp.where(lanes_low(y.shape), one, two)
        other = swap_halves(y)
        low = lanes_low(y.shape)
        y1[2 * t] = jnp.where(low, y, other)
        y1[2 * t + 1] = jnp.where(low, other, y)

    def down(m, _):
        for u in range(2):
            t = 2 * m + u
            at = pl.ds(pl.multiple_of(t * 128, 128), 128)
            y = coupled(
                [[source_of(far0_ref[f, 2 * t + i], place, LEAF) for f in range(FAR0)] for i in range(2)],
                [c0[f, :, at] for f in range(FAR0)], q_low, q_high,
            )
            w = t1[:, at]
            one, two = transposed(*halves(y1[m]), jnp.concatenate([w, w], axis=0))
            y = y + jnp.where(lanes_low(y.shape), one, two)
            one, two = transposed(*halves(y), basis[:, at])
            acc[2 * t] += one
            acc[2 * t + 1] += two
        return 0

    lax.fori_loop(0, MID, down, 0)

    swaps[0].wait()
    for leaf in range(LEAF):
        prepare(p1, x1, leaf, LEAF + leaf, eye, centres, feats, xs)
    outs = [
        pltpu.make_async_copy(src, dst, out_sem.at[i])
        for i, (src, dst) in enumerate(
            [
                (acc, acc_out), (pack, pack_out), (p2, p2_ref), (centres.at[0:48], centres_out),
                (feats.at[0:24], feats_out.at[0:24]), (feats.at[24:48], feats_out.at[24:48]),
                (xs.at[0:24], xs_out.at[0:24]), (xs.at[24:48], xs_out.at[24:48]),
            ]
        )
    ]
    for c in outs:
        c.start()
    for d in range(1, GROUPS):
        part_copy(d)[0].wait_send()
    for d in range(1, LANES):
        y2_copy(d)[0].wait_send()

    swaps[1].wait()
    swaps[4].wait()
    for c in outs:
        c.wait()


def rest_kernel(
    list_ref, own_hbm, p2_hbm, x2_hbm, acc_hbm, centres_hbm, feats_hbm, xs_hbm, out_ref,
    own, p2, targets, centres, feats, xs, acc, x, sem, out_sem,
):
    moves = [
        pltpu.make_async_copy(src, dst, sem.at[i])
        for i, (src, dst) in enumerate(
            [(own_hbm, own), (p2_hbm, p2)]
            + [(x2_hbm.at[:, c * 1536:c * 1536 + 1536], x.at[:, c * 1536:c * 1536 + 1536]) for c in range(4)]
            + [
                (acc_hbm, acc.at[0:24]), (centres_hbm, centres.at[0:48]),
                (feats_hbm.at[0:24], feats.at[0:24]), (feats_hbm.at[24:48], feats.at[24:48]),
                (xs_hbm.at[0:24], xs.at[0:24]), (xs_hbm.at[24:48], xs.at[24:48]),
            ]
        )
    ]
    for c in moves[:6]:
        c.start()
    targets[LEAF] = jnp.zeros((8, PTS), f32)
    acc[LEAF] = jnp.zeros((64, PTS), f32)
    eye = identity()
    for c in moves[:6]:
        c.wait()
    for c in moves[6:]:
        c.start()
    for leaf in range(LEAF):
        targets[leaf] = leaf_rows(own, leaf)
        prepare(p2, x, leaf, 2 * LEAF + leaf, eye, centres, feats, xs)
    for c in moves[6:]:
        c.wait()

    @pl.loop(0, (list_ref[COUNT_ROW, 0] + (UNROLL - 1)) // UNROLL)
    def _(i):
        words = [list_ref[REST_ROW, i * UNROLL + u] for u in range(UNROLL)]
        pairs(
            [lax.shift_right_logical(w, 7) for w in words], [w & 127 for w in words], targets, centres, feats, xs, acc
        )

    outs = [
        pltpu.make_async_copy(acc.at[leaf], out_ref.at[:, leaf * PTS:leaf * PTS + PTS], out_sem.at[leaf])
        for leaf in range(LEAF)
    ]
    for c in outs:
        c.start()
    for c in outs:
        c.wait()


VM = pl.BlockSpec(memory_space=pltpu.VMEM)
SM = pl.BlockSpec(memory_space=pltpu.SMEM)
ANY = pl.BlockSpec(memory_space=pl.ANY)
DMA = pltpu.SemaphoreType.DMA


def params(mib, **more):
    return pltpu.CompilerParams(vmem_limit_bytes=mib << 20, **more)


def cost(size):
    return pl.CostEstimate(flops=size, bytes_accessed=1000, transcendentals=0)


def shape(*dims, dtype=f32):
    return jax.ShapeDtypeStruct(dims, dtype)


def local(
    coords, charges, basis, transfer1, transfer2, coupling0, coupling1, coupling2, near_list, near_count, far0_list,
    far1_list, far2_list,
):
    lists = pl.pallas_call(
        list_kernel, out_shape=shape(16, PTS, dtype=jnp.int32), in_specs=[VM, VM], out_specs=VM,
        compiler_params=params(56), cost_estimate=cost(1000), name="lists",
    )(near_list.T, near_count.reshape(1, LEAF))
    wide = LEAF * PTS
    acc, pack, p2, x2, centres, feats, xs = pl.pallas_call(
        main_kernel,
        out_shape=(
            shape(LEAF, 64, PTS), shape(18, 64, 128), shape(18, 64, 128), shape(64, wide), shape(2 * LEAF, 8, PTS),
            shape(2 * LEAF, PTS, 128, dtype=bf16), shape(2 * LEAF, 128, PTS, dtype=bf16),
        ),
        in_specs=[SM] * 4 + [ANY] * 8,
        out_specs=(ANY,) * 7,
        scratch_shapes=[
            pltpu.VMEM((3, wide), f32), pltpu.VMEM((64, wide), f32), pltpu.VMEM((64, wide), f32),
            pltpu.VMEM((PTS, LEAF * RANK), f32), pltpu.VMEM((RANK, LEAF * RANK), f32),
            pltpu.VMEM((RANK, MID * RANK), f32), pltpu.VMEM((FAR0, RANK, LEAF * RANK), f32),
            pltpu.VMEM((FAR1, RANK, MID * RANK), f32), pltpu.VMEM((FAR2, RANK, RANK), f32),
            pltpu.VMEM((18, 64, 128), f32), pltpu.VMEM((18, 64, 128), f32), pltpu.VMEM((18, 64, 128), f32),
            pltpu.VMEM((LEAF, 64, PTS), f32), pltpu.VMEM((LEAF, 8, PTS), f32),
            pltpu.VMEM((2 * LEAF + 1, 8, PTS), f32), pltpu.VMEM((2 * LEAF + 1, PTS, 128), bf16),
            pltpu.VMEM((2 * LEAF + 1, 128, PTS), bf16),
            pltpu.VMEM((32, 128), f32), pltpu.VMEM((GROUPS, 32, 128), f32), pltpu.VMEM((32, 128), f32),
            pltpu.VMEM((LANES, 32, 128), f32), pltpu.VMEM((MID, 64, 128), f32),
            pltpu.VMEM((3 * LEAF, 128, 128), bf16), pltpu.VMEM((3 * LEAF, 128, 128), bf16),
            pltpu.VMEM((3 * MID, 128, 128), bf16), pltpu.VMEM((3 * MID, 128, 128), bf16),
            DMA((17,)), DMA((GROUPS,)), DMA((GROUPS,)), DMA((LANES,)), DMA((LANES,)), DMA((5,)), DMA((5,)),
            DMA((8,)),
        ],
        compiler_params=params(56, collective_id=0, has_side_effects=True),
        cost_estimate=cost(1000),
        name="main",
    )(
        lists, far0_list.T, far1_list.T, far2_list.T, coords, charges, basis, transfer1, transfer2, coupling0,
        coupling1, coupling2,
    )
    return pl.pallas_call(
        rest_kernel,
        out_shape=shape(64, wide),
        in_specs=[SM] + [ANY] * 7,
        out_specs=ANY,
        scratch_shapes=[
            pltpu.VMEM((18, 64, 128), f32), pltpu.VMEM((18, 64, 128), f32), pltpu.VMEM((LEAF + 1, 8, PTS), f32),
            pltpu.VMEM((3 * LEAF, 8, PTS), f32), pltpu.VMEM((3 * LEAF, PTS, 128), bf16),
            pltpu.VMEM((3 * LEAF, 128, PTS), bf16), pltpu.VMEM((LEAF + 1, 64, PTS), f32), pltpu.VMEM((64, wide), f32),
            DMA((12,)), DMA((LEAF,)),
        ],
        compiler_params=params(56),
        cost_estimate=cost(1000),
        name="rest",
    )(lists, pack, p2, x2, acc, centres, feats, xs)


def solution(mesh):
    placed = (
        P(None, AXES),
        P(None, AXES),
        P(None, AXES),
        P(None, AXES),
        P(None, AXES),
        P(None, None, AXES),
        P(None, None, AXES),
        P(None, None, "grp"),
        P(AXES, None),
        P(AXES),
        P(AXES, None),
        P(AXES, None),
        P(),
    )
    return jax.shard_map(local, mesh=mesh, in_specs=placed, out_specs=P(None, AXES), check_vma=False)
```

```python
import math

import jax
import jax.numpy as jnp
from jax import lax
from jax.experimental import pallas as pl
from jax.experimental.pallas import tpu as pltpu
from jax.sharding import PartitionSpec as P

AXES = ("grp", "lane")
LANES = 8
DEVS = 128
LEAF = 24
MID = 6
PTS = 256
RANK = 64
NEAR = 9
FAR0 = 8
FAR1 = 4
FAR2 = 4
UNROLL = 24
SLOTS = 5
REST_ROW = 8
COUNT_ROW = 9
STEP = 4
GROUPS = 16
MESH = pl.DeviceIdType.MESH
inv_four_pi = 1.0 / (4.0 * math.pi)
smooth_sq = 5e-05
bf16 = jnp.bfloat16
f32 = jnp.float32
NT = (((1,), (1,)), ((), ()))


def dot(a, b, dims=(((1,), (0,)), ((), ()))):
    return lax.dot_general(a, b, dims, preferred_element_type=f32)


def split(a):
    high = a.astype(bf16)
    return high, (a - high.astype(f32)).astype(bf16)


def lanes_low(shape):
    return lax.broadcasted_iota(jnp.int32, shape, len(shape) - 1) < RANK


def swap_halves(a):
    return pltpu.roll(a, RANK, 1)


def halves(tile):
    low = lanes_low(tile.shape)
    return jnp.where(low, tile, 0.0), jnp.where(low, 0.0, tile)


def place_of():
    return lax.axis_index("grp") * LANES + lax.axis_index("lane")


def source_of(entry, place, width):
    even = lax.rem(place, 2) == 0
    rel = entry - place * width
    rel = jnp.where(rel < -width, rel + DEVS * width, jnp.where(rel >= 2 * width, rel - DEVS * width, rel))
    low_off = jnp.where(even, 3 * width, 2 * width)
    high_off = jnp.where(even, 0, width)
    source = rel + jnp.where(rel < 0, low_off, jnp.where(rel >= width, high_off, 0))
    return jnp.minimum(jnp.maximum(source, 0), 3 * width - 1)


def stacked_split(rows_a, rows_b):
    ah, al = split(rows_a)
    bh, bl = split(rows_b)
    return jnp.concatenate([ah, bh, al, bl], axis=0)


def wide_split(a):
    h, l = split(a)
    return jnp.concatenate([h, l], axis=1)


def fold(out):
    s = out[:, :128] + out[:, 128:]
    return s[0:64] + s[128:192], s[64:128] + s[192:256]


def transposed(rows_a, rows_b, weights):
    lhs = stacked_split(rows_a, rows_b)
    wh, wl = split(weights)
    r = dot(lhs, wh, NT)
    r2 = dot(lhs[:128], wl, NT)
    return r[0:64] + r[128:192] + r2[0:64], r[64:128] + r[192:256] + r2[64:128]


def list_kernel(near_ref, count_ref, out_ref):
    place = place_of()
    source = source_of(near_ref[...], place, LEAF)
    count = count_ref[...]
    leaf = lax.broadcasted_iota(jnp.int32, (1, LEAF), 1)
    own_at = jnp.zeros((1, LEAF), jnp.int32)
    rest_at = jnp.zeros((1, LEAF), jnp.int32)
    own = [jnp.full((1, LEAF), LEAF, jnp.int32) for _ in range(SLOTS - 1)]
    places = []
    for k in range(1, NEAR):
        src = source[k:k + 1]
        live = count > k
        here = jnp.logical_and(jnp.logical_and(src < LEAF, live), own_at < SLOTS - 1)
        for s in range(SLOTS - 1):
            own[s] = jnp.where(jnp.logical_and(here, own_at == s), src, own[s])
        own_at = own_at + jnp.where(here, 1, 0)
        rest = jnp.logical_and(live, jnp.logical_not(here))
        places.append((rest, rest_at))
        rest_at = rest_at + jnp.where(rest, 1, 0)
    row = lax.broadcasted_iota(jnp.int32, (LEAF, LEAF), 0)
    col = lax.broadcasted_iota(jnp.int32, (LEAF, LEAF), 1)
    before = jnp.where(row < col, 1.0, 0.0).astype(bf16)
    counts = jnp.broadcast_to(rest_at.astype(f32), (16, LEAF)).astype(bf16)
    base = dot(counts, before)[0:1]
    at = [jnp.where(rest, base + pos.astype(f32), -1.0) for rest, pos in places]
    values = jnp.concatenate(at + [source[k:k + 1].astype(f32) for k in range(1, NEAR)], axis=0).astype(bf16)
    columns = dot(jnp.where(row == col, 1.0, 0.0).astype(bf16), values, NT)
    lanes = lax.broadcasted_iota(jnp.int32, (LEAF, PTS), 1).astype(f32)
    word = lax.broadcasted_iota(jnp.int32, (LEAF, 1), 0).astype(f32) * 128.0
    flat = jnp.zeros((LEAF, PTS), f32)
    for k in range(NEAR - 1):
        flat = flat + jnp.where(columns[:, k:k + 1] == lanes, word + columns[:, NEAR - 1 + k:NEAR + k], 0.0)
    flat = jnp.sum(flat, axis=0, keepdims=True)
    total = jnp.sum(rest_at.astype(f32), axis=1, keepdims=True)
    flat = jnp.where(lanes[0:1] < total, flat, LEAF * 128.0)
    out_ref[...] = jnp.zeros((16, PTS), jnp.int32)
    out_ref[0:1, 0:LEAF] = leaf
    for s in range(SLOTS - 1):
        out_ref[s + 1:s + 2, 0:LEAF] = own[s]
    out_ref[REST_ROW:REST_ROW + 1, :] = flat.astype(jnp.int32)
    out_ref[COUNT_ROW:COUNT_ROW + 1, :] = jnp.broadcast_to(total, (1, PTS)).astype(jnp.int32)


def upward(coords_ref, x_ref, basis_ref, t1_ref, t2_ref, pack_ref):
    tiles = []
    for t in range(LEAF // 2):
        xa = x_ref[:, t * 512:t * 512 + 256]
        xb = x_ref[:, t * 512 + 256:t * 512 + 512]
        ra, rb = fold(dot(stacked_split(xa, xb), wide_split(basis_ref[:, t * 128:t * 128 + 128])))
        q = jnp.where(lanes_low(ra.shape), ra, rb)
        pack_ref[t] = q
        tiles.append(q)
    mids = []
    parts = []
    for m in range(MID):
        a0, b0 = halves(tiles[2 * m])
        a1, b1 = halves(tiles[2 * m + 1])
        e0 = t1_ref[:, m * 256:m * 256 + 128]
        e1 = t1_ref[:, m * 256 + 128:m * 256 + 256]
        lhs = stacked_split(jnp.concatenate([a0, a1], axis=1), jnp.concatenate([b0, b1], axis=1))
        parts.append(fold(dot(lhs, wide_split(jnp.concatenate([e0, e0, e1, e1], axis=0)))))
    for t in range(MID // 2):
        (top0, bot0), (top1, bot1) = parts[2 * t], parts[2 * t + 1]
        low = lanes_low(top0.shape)
        mid = jnp.where(low, top0, bot1) + swap_halves(jnp.where(low, top1, bot0))
        pack_ref[LEAF // 2 + t] = mid
        mids.append(mid)
    both = [halves(m) for m in mids]
    weights = [t2_ref[:, t * 128:t * 128 + 128] for t in range(MID // 2)]
    lhs = stacked_split(
        jnp.concatenate([b[0] for b in both], axis=1), jnp.concatenate([b[1] for b in both], axis=1)
    )
    top, bot = fold(dot(lhs, wide_split(jnp.concatenate([w for w in weights for _ in range(2)], axis=0))))
    for i in range(2 * LEAF):
        for c in range(3):
            pack_ref[15 + c, i:i + 1, :] = coords_ref[c:c + 1, i * 128:i * 128 + 128]
    zero = jnp.zeros((16, 128), f32)
    for c in range(3):
        pack_ref[15 + c, 48:64, :] = zero
    s = jnp.where(lanes_low(top.shape), top, bot)
    return s + swap_halves(s)


def leaf_rows(pack_ref, leaf):
    row = lax.broadcasted_iota(jnp.int32, (8, PTS), 0)
    out = jnp.zeros((8, PTS), f32)
    for c in range(3):
        line = jnp.concatenate(
            [pack_ref[15 + c, 2 * leaf:2 * leaf + 1, :], pack_ref[15 + c, 2 * leaf + 1:2 * leaf + 2, :]], axis=1
        )
        out = jnp.where(row == c, line, out)
    return out


def pieces(a):
    h = a.astype(bf16).astype(f32)
    r = a - h
    m = r.astype(bf16).astype(f32)
    return h, m, r - m


def identity():
    return jnp.where(
        lax.broadcasted_iota(jnp.int32, (PTS, PTS), 0) == lax.broadcasted_iota(jnp.int32, (PTS, PTS), 1), 1.0, 0.0
    ).astype(bf16)


def prepare(pack_ref, x_ref, leaf, at, eye, centres, feats, xs):
    row = lax.broadcasted_iota(jnp.int32, (8, PTS), 0)
    source = leaf_rows(pack_ref, leaf)
    centre = jnp.broadcast_to(jnp.sum(source, axis=1, keepdims=True) * (1.0 / PTS), (8, PTS))
    centres[at] = centre
    d = source - centre
    sq = jnp.sum(d * d, axis=0, keepdims=True) + smooth_sq
    h, m, l = pieces(jnp.where(row < 3, -2.0 * d, jnp.where(row == 3, 1.0, jnp.where(row == 4, sq, 0.0))))
    rows = jnp.concatenate([h, m, h, l, m, h, jnp.zeros((80, PTS), f32)], axis=0).astype(bf16)
    feats[at] = dot(eye, rows, NT).astype(bf16)
    xh, xl = split(x_ref[:, leaf * PTS:leaf * PTS + PTS] * inv_four_pi)
    xs[at] = jnp.concatenate([xh, xl], axis=0)


def pairs(ls, js, targets, centres, feats, xs, acc):
    unit = jnp.where(lax.broadcasted_iota(jnp.int32, (8, PTS), 0) == 4, 1.0, 0.0)
    row = lax.broadcasted_iota(jnp.int32, (8, PTS), 0)
    dist = []
    for l, j in zip(ls, js):
        d = targets[l] - centres[j]
        sq = jnp.sum(d * d, axis=0, keepdims=True)
        h, m, low = pieces(jnp.where(row == 3, sq, d + unit))
        rows = jnp.concatenate([h, h, m, h, m, low], axis=0).astype(bf16)
        dist.append(dot(feats[j][:, :48], rows))
    for l, j, d2 in zip(ls, js, dist):
        kh, kl = split(lax.rsqrt(d2))
        x = xs[j]
        r = dot(x, kh) + dot(x, kl)
        acc[l] += r[:64] + r[64:]


def place_tile(tile, low_ref, high_ref, at):
    other = swap_halves(tile)
    low = lanes_low(tile.shape)
    for i, (here, there) in enumerate(((tile, other), (other, tile))):
        h, l = split(jnp.where(low, here, 0.0))
        low_ref[at + i] = jnp.concatenate([h, l], axis=0)
        h, l = split(jnp.where(low, 0.0, there))
        high_ref[at + i] = jnp.concatenate([h, l], axis=0)


def coupled(sources, weights, low_ref, high_ref):
    lhs = jnp.concatenate(
        [
            jnp.concatenate([low_ref[row[f]] + high_ref[row[f + 1]] for f in range(0, len(row), 2)], axis=1)
            for row in sources
        ],
        axis=0,
    )
    out = dot(lhs, wide_split(jnp.concatenate(weights, axis=0)))
    s = out[:, :128] + out[:, 128:]
    even, odd = s[0:64] + s[64:128], s[128:192] + s[192:256]
    return jnp.where(lanes_low(even.shape), even, odd)


def top_coupled(picks, c2_ref):
    tiles = []
    for f in range(0, FAR2, 2):
        a = jnp.concatenate([picks[f], swap_halves(picks[f])], axis=0)
        b = jnp.concatenate([swap_halves(picks[f + 1]), picks[f + 1]], axis=0)
        tiles.append(jnp.where(lanes_low(a.shape), a, b))
    th, tl = split(jnp.concatenate(tiles, axis=1))
    w = jnp.concatenate([c2_ref[f] for f in range(FAR2)], axis=0)
    wh, wl = split(jnp.concatenate([w, w], axis=1))
    y2 = dot(th, wh) + dot(tl, wh) + dot(th, wl)
    return jnp.where(lanes_low((32, 128)), y2[:32], y2[32:])


def main_kernel(
    list_ref, far0_ref, far1_ref, far2_ref, coords_hbm, x_hbm, basis_hbm, t1_hbm, t2_hbm, c0_hbm, c1_hbm, c2_hbm,
    acc_out, pack_out, p2_ref, x2_ref, centres_out, feats_out, xs_out,
    coords, x, x1, basis, t1, t2, c0, c1, c2, pack, p1, p2, acc, targets, centres, feats, xs,
    part, parts, y2_part, y2_parts, y1, q_low, q_high, m_low, m_high,
    load_sem, part_send, part_recv, y2_send, y2_recv, swap_send, swap_recv, out_sem,
):
    group = lax.axis_index("grp")
    lane = lax.axis_index("lane")
    place = group * LANES + lane
    even = lax.rem(lane, 2) == 0
    partner = (group, lane + 1 - 2 * lax.rem(lane, 2))
    beyond = lax.rem(place + jnp.where(even, DEVS - 1, 1), DEVS)
    beyond = (beyond // LANES, lax.rem(beyond, LANES))

    barrier = pltpu.get_barrier_semaphore()
    for d in range(1, LANES):
        pl.semaphore_signal(barrier, inc=1, device_id=(group, lax.rem(lane + d, LANES)), device_id_type=MESH)
    for d in range(1, GROUPS):
        pl.semaphore_signal(barrier, inc=1, device_id=(lax.rem(group + d, GROUPS), lane), device_id_type=MESH)
    pl.semaphore_signal(barrier, inc=1, device_id=beyond, device_id_type=MESH)

    loads = [
        pltpu.make_async_copy(src, dst, load_sem.at[i])
        for i, (src, dst) in enumerate(
            [(x_hbm.at[:, c * 1536:c * 1536 + 1536], x.at[:, c * 1536:c * 1536 + 1536]) for c in range(4)]
            + [(basis_hbm.at[r * 64:r * 64 + 64], basis.at[r * 64:r * 64 + 64]) for r in range(4)]
            + [(t1_hbm, t1), (t2_hbm, t2), (coords_hbm, coords)]
            + [(c0_hbm.at[r * 2:r * 2 + 2], c0.at[r * 2:r * 2 + 2]) for r in range(4)]
            + [(c1_hbm, c1), (c2_hbm, c2)]
        )
    ]
    for c in loads:
        c.start()
    for c in loads[:11]:
        c.wait()
    top = upward(coords, x, basis, t1, t2, pack)
    part[...] = jnp.where(lanes_low((32, 128)), top[:32], top[32:])
    pl.semaphore_wait(barrier, LANES + GROUPS - 1)

    def part_copy(d):
        peer = lax.rem(group + d, GROUPS)
        return (
            pltpu.make_async_remote_copy(
                part, parts.at[group], part_send.at[d], part_recv.at[group], (peer, lane), MESH
            ),
            pltpu.make_async_remote_copy(
                part, parts.at[peer], part_send.at[d], part_recv.at[peer], (peer, lane), MESH
            ),
        )

    def y2_copy(d):
        peer = lax.rem(lane + d, LANES)
        return (
            pltpu.make_async_remote_copy(
                y2_part, y2_parts.at[lane], y2_send.at[d], y2_recv.at[lane], (group, peer), MESH
            ),
            pltpu.make_async_remote_copy(
                y2_part, y2_parts.at[peer], y2_send.at[d], y2_recv.at[peer], (group, peer), MESH
            ),
        )

    def swap(src, dst, i, device):
        return pltpu.make_async_remote_copy(src, dst, swap_send.at[i], swap_recv.at[i], device, MESH)

    swaps = [
        swap(pack, p2, 0, beyond),
        swap(pack, p1, 1, partner),
        swap(x, x1, 2, partner),
        swap(x, x2_ref, 3, beyond),
    ]
    for d in range(1, GROUPS):
        part_copy(d)[0].start()
    for c in swaps[:3]:
        c.start()

    eye = identity()
    for leaf in range(LEAF):
        targets[leaf] = leaf_rows(pack, leaf)
        prepare(pack, x, leaf, leaf, eye, centres, feats, xs)
        acc[leaf] = jnp.zeros((64, PTS), f32)
    centres[2 * LEAF] = jnp.zeros((8, PTS), f32)
    feats[2 * LEAF] = feats[0]
    xs[2 * LEAF] = jnp.zeros((128, PTS), bf16)

    def leaves(i, _):
        at = [STEP * i + u for u in range(STEP) for s in range(SLOTS)]
        js = [list_ref[s, STEP * i + u] for u in range(STEP) for s in range(SLOTS)]
        pairs(at, [jnp.where(j == LEAF, 2 * LEAF, j) for j in js], targets, centres, feats, xs, acc)
        return 0

    lax.fori_loop(0, 2, leaves, 0)

    for c in loads[11:]:
        c.wait()
    for d in range(1, GROUPS):
        part_copy(d)[1].wait_recv()
    parts[group] = part[...]
    mine = top_coupled([parts[far2_ref[f, group]] for f in range(FAR2)], c2)
    y2_part[...] = mine
    y2_parts[lane] = mine
    for d in range(1, LANES):
        y2_copy(d)[0].start()

    lax.fori_loop(2, 4, leaves, 0)

    for c in swaps[:2]:
        c.wait()
    for d in range(1, LANES):
        y2_copy(d)[1].wait_recv()
    swaps[3].start()

    lax.fori_loop(4, LEAF // STEP, leaves, 0)

    for b, p in enumerate((pack, p1, p2)):
        for t in range(LEAF // 2):
            place_tile(p[t], q_low, q_high, LEAF * b + 2 * t)
        for t in range(MID // 2):
            place_tile(p[LEAF // 2 + t], m_low, m_high, MID * b + 2 * t)
    y2 = y2_parts[0]
    for r in range(1, LANES):
        y2 = y2 + y2_parts[r]
    other = swap_halves(y2)
    low = lanes_low(y2.shape)
    y2 = jnp.concatenate([jnp.where(low, y2, other), jnp.where(low, other, y2)], axis=0)

    for t in range(MID // 2):
        at = slice(t * 128, t * 128 + 128)
        y = coupled(
            [[source_of(far1_ref[f, 2 * t + i], place, MID) for f in range(FAR1)] for i in range(2)],
            [c1[f, :, at] for f in range(FAR1)], m_low, m_high,
        )
        w = t2[:, at]
        one, two = transposed(*halves(y2), jnp.concatenate([w, w], axis=0))
        y = y + jnp.where(lanes_low(y.shape), one, two)
        other = swap_halves(y)
        low = lanes_low(y.shape)
        y1[2 * t] = jnp.where(low, y, other)
        y1[2 * t + 1] = jnp.where(low, other, y)

    def down(m, _):
        for u in range(2):
            t = 2 * m + u
            at = pl.ds(pl.multiple_of(t * 128, 128), 128)
            y = coupled(
                [[source_of(far0_ref[f, 2 * t + i], place, LEAF) for f in range(FAR0)] for i in range(2)],
                [c0[f, :, at] for f in range(FAR0)], q_low, q_high,
            )
            w = t1[:, at]
            one, two = transposed(*halves(y1[m]), jnp.concatenate([w, w], axis=0))
            y = y + jnp.where(lanes_low(y.shape), one, two)
            one, two = transposed(*halves(y), basis[:, at])
            acc[2 * t] += one
            acc[2 * t + 1] += two
        return 0

    lax.fori_loop(0, MID, down, 0)

    swaps[2].wait()
    for leaf in range(LEAF):
        prepare(p1, x1, leaf, LEAF + leaf, eye, centres, feats, xs)
    outs = [
        pltpu.make_async_copy(src, dst, out_sem.at[i])
        for i, (src, dst) in enumerate(
            [
                (acc, acc_out), (pack, pack_out), (p2, p2_ref), (centres.at[0:48], centres_out),
                (feats.at[0:24], feats_out.at[0:24]), (feats.at[24:48], feats_out.at[24:48]),
                (xs.at[0:24], xs_out.at[0:24]), (xs.at[24:48], xs_out.at[24:48]),
            ]
        )
    ]
    for c in outs:
        c.start()
    for d in range(1, GROUPS):
        part_copy(d)[0].wait_send()
    for d in range(1, LANES):
        y2_copy(d)[0].wait_send()

    swaps[3].wait()
    for c in outs:
        c.wait()


def rest_kernel(
    list_ref, own_hbm, p2_hbm, x2_hbm, acc_hbm, centres_hbm, feats_hbm, xs_hbm, out_ref,
    own, p2, targets, centres, feats, xs, acc, x, sem, out_sem,
):
    moves = [
        pltpu.make_async_copy(src, dst, sem.at[i])
        for i, (src, dst) in enumerate(
            [(own_hbm, own), (p2_hbm, p2)]
            + [(x2_hbm.at[:, c * 1536:c * 1536 + 1536], x.at[:, c * 1536:c * 1536 + 1536]) for c in range(4)]
            + [
                (acc_hbm, acc.at[0:24]), (centres_hbm, centres.at[0:48]),
                (feats_hbm.at[0:24], feats.at[0:24]), (feats_hbm.at[24:48], feats.at[24:48]),
                (xs_hbm.at[0:24], xs.at[0:24]), (xs_hbm.at[24:48], xs.at[24:48]),
            ]
        )
    ]
    for c in moves[:6]:
        c.start()
    targets[LEAF] = jnp.zeros((8, PTS), f32)
    acc[LEAF] = jnp.zeros((64, PTS), f32)
    eye = identity()
    for c in moves[:6]:
        c.wait()
    for c in moves[6:]:
        c.start()
    for leaf in range(LEAF):
        targets[leaf] = leaf_rows(own, leaf)
        prepare(p2, x, leaf, 2 * LEAF + leaf, eye, centres, feats, xs)
    for c in moves[6:]:
        c.wait()

    @pl.loop(0, (list_ref[COUNT_ROW, 0] + (UNROLL - 1)) // UNROLL)
    def _(i):
        words = [list_ref[REST_ROW, i * UNROLL + u] for u in range(UNROLL)]
        pairs(
            [lax.shift_right_logical(w, 7) for w in words], [w & 127 for w in words], targets, centres, feats, xs, acc
        )

    outs = [
        pltpu.make_async_copy(acc.at[leaf], out_ref.at[:, leaf * PTS:leaf * PTS + PTS], out_sem.at[leaf])
        for leaf in range(LEAF)
    ]
    for c in outs:
        c.start()
    for c in outs:
        c.wait()


VM = pl.BlockSpec(memory_space=pltpu.VMEM)
SM = pl.BlockSpec(memory_space=pltpu.SMEM)
ANY = pl.BlockSpec(memory_space=pl.ANY)
DMA = pltpu.SemaphoreType.DMA


def params(mib, **more):
    return pltpu.CompilerParams(vmem_limit_bytes=mib << 20, **more)


def cost(size):
    return pl.CostEstimate(flops=size, bytes_accessed=1000, transcendentals=0)


def shape(*dims, dtype=f32):
    return jax.ShapeDtypeStruct(dims, dtype)


def local(
    coords, charges, basis, transfer1, transfer2, coupling0, coupling1, coupling2, near_list, near_count, far0_list,
    far1_list, far2_list,
):
    lists = pl.pallas_call(
        list_kernel, out_shape=shape(16, PTS, dtype=jnp.int32), in_specs=[VM, VM], out_specs=VM,
        compiler_params=params(56), cost_estimate=cost(1000), name="lists",
    )(near_list.T, near_count.reshape(1, LEAF))
    wide = LEAF * PTS
    acc, pack, p2, x2, centres, feats, xs = pl.pallas_call(
        main_kernel,
        out_shape=(
            shape(LEAF, 64, PTS), shape(18, 64, 128), shape(18, 64, 128), shape(64, wide), shape(2 * LEAF, 8, PTS),
            shape(2 * LEAF, PTS, 128, dtype=bf16), shape(2 * LEAF, 128, PTS, dtype=bf16),
        ),
        in_specs=[SM] * 4 + [ANY] * 8,
        out_specs=(ANY,) * 7,
        scratch_shapes=[
            pltpu.VMEM((3, wide), f32), pltpu.VMEM((64, wide), f32), pltpu.VMEM((64, wide), f32),
            pltpu.VMEM((PTS, LEAF * RANK), f32), pltpu.VMEM((RANK, LEAF * RANK), f32),
            pltpu.VMEM((RANK, MID * RANK), f32), pltpu.VMEM((FAR0, RANK, LEAF * RANK), f32),
            pltpu.VMEM((FAR1, RANK, MID * RANK), f32), pltpu.VMEM((FAR2, RANK, RANK), f32),
            pltpu.VMEM((18, 64, 128), f32), pltpu.VMEM((18, 64, 128), f32), pltpu.VMEM((18, 64, 128), f32),
            pltpu.VMEM((LEAF, 64, PTS), f32), pltpu.VMEM((LEAF, 8, PTS), f32),
            pltpu.VMEM((2 * LEAF + 1, 8, PTS), f32), pltpu.VMEM((2 * LEAF + 1, PTS, 128), bf16),
            pltpu.VMEM((2 * LEAF + 1, 128, PTS), bf16),
            pltpu.VMEM((32, 128), f32), pltpu.VMEM((GROUPS, 32, 128), f32), pltpu.VMEM((32, 128), f32),
            pltpu.VMEM((LANES, 32, 128), f32), pltpu.VMEM((MID, 64, 128), f32),
            pltpu.VMEM((3 * LEAF, 128, 128), bf16), pltpu.VMEM((3 * LEAF, 128, 128), bf16),
            pltpu.VMEM((3 * MID, 128, 128), bf16), pltpu.VMEM((3 * MID, 128, 128), bf16),
            DMA((17,)), DMA((GROUPS,)), DMA((GROUPS,)), DMA((LANES,)), DMA((LANES,)), DMA((4,)), DMA((4,)),
            DMA((8,)),
        ],
        compiler_params=params(56, collective_id=0, has_side_effects=True),
        cost_estimate=cost(1000),
        name="main",
    )(
        lists, far0_list.T, far1_list.T, far2_list.T, coords, charges, basis, transfer1, transfer2, coupling0,
        coupling1, coupling2,
    )
    return pl.pallas_call(
        rest_kernel,
        out_shape=shape(64, wide),
        in_specs=[SM] + [ANY] * 7,
        out_specs=ANY,
        scratch_shapes=[
            pltpu.VMEM((18, 64, 128), f32), pltpu.VMEM((18, 64, 128), f32), pltpu.VMEM((LEAF + 1, 8, PTS), f32),
            pltpu.VMEM((3 * LEAF, 8, PTS), f32), pltpu.VMEM((3 * LEAF, PTS, 128), bf16),
            pltpu.VMEM((3 * LEAF, 128, PTS), bf16), pltpu.VMEM((LEAF + 1, 64, PTS), f32), pltpu.VMEM((64, wide), f32),
            DMA((12,)), DMA((LEAF,)),
        ],
        compiler_params=params(56),
        cost_estimate=cost(1000),
        name="rest",
    )(lists, pack, p2, x2, acc, centres, feats, xs)


def solution(mesh):
    placed = (
        P(None, AXES),
        P(None, AXES),
        P(None, AXES),
        P(None, AXES),
        P(None, AXES),
        P(None, None, AXES),
        P(None, None, AXES),
        P(None, None, "grp"),
        P(AXES, None),
        P(AXES),
        P(AXES, None),
        P(AXES, None),
        P(),
    )
    return jax.shard_map(local, mesh=mesh, in_specs=placed, out_specs=P(None, AXES), check_vma=False)
```

```python
import math

import jax
import jax.numpy as jnp
from jax import lax
from jax.experimental import pallas as pl
from jax.experimental.pallas import tpu as pltpu
from jax.sharding import PartitionSpec as P

AXES = ("grp", "lane")
LANES = 8
DEVS = 128
LEAF = 24
MID = 6
PTS = 256
RANK = 64
NEAR = 9
FAR0 = 8
FAR1 = 4
FAR2 = 4
UNROLL = 24
SLOTS = 5
REST_ROW = 8
COUNT_ROW = 9
STEP = 4
GROUPS = 16
MESH = pl.DeviceIdType.MESH
inv_four_pi = 1.0 / (4.0 * math.pi)
smooth_sq = 5e-05
bf16 = jnp.bfloat16
f32 = jnp.float32
NT = (((1,), (1,)), ((), ()))


def dot(a, b, dims=(((1,), (0,)), ((), ()))):
    return lax.dot_general(a, b, dims, preferred_element_type=f32)


def split(a):
    high = a.astype(bf16)
    return high, (a - high.astype(f32)).astype(bf16)


def lanes_low(shape):
    return lax.broadcasted_iota(jnp.int32, shape, len(shape) - 1) < RANK


def swap_halves(a):
    return pltpu.roll(a, RANK, 1)


def halves(tile):
    low = lanes_low(tile.shape)
    return jnp.where(low, tile, 0.0), jnp.where(low, 0.0, tile)


def place_of():
    return lax.axis_index("grp") * LANES + lax.axis_index("lane")


def source_of(entry, place, width):
    even = lax.rem(place, 2) == 0
    rel = entry - place * width
    rel = jnp.where(rel < -width, rel + DEVS * width, jnp.where(rel >= 2 * width, rel - DEVS * width, rel))
    low_off = jnp.where(even, 3 * width, 2 * width)
    high_off = jnp.where(even, 0, width)
    source = rel + jnp.where(rel < 0, low_off, jnp.where(rel >= width, high_off, 0))
    return jnp.minimum(jnp.maximum(source, 0), 3 * width - 1)


def stacked_split(rows_a, rows_b):
    ah, al = split(rows_a)
    bh, bl = split(rows_b)
    return jnp.concatenate([ah, bh, al, bl], axis=0)


def wide_split(a):
    h, l = split(a)
    return jnp.concatenate([h, l], axis=1)


def fold(out):
    s = out[:, :128] + out[:, 128:]
    return s[0:64] + s[128:192], s[64:128] + s[192:256]


def transposed(rows_a, rows_b, weights):
    lhs = stacked_split(rows_a, rows_b)
    wh, wl = split(weights)
    r = dot(lhs, wh, NT)
    r2 = dot(lhs[:128], wl, NT)
    return r[0:64] + r[128:192] + r2[0:64], r[64:128] + r[192:256] + r2[64:128]


def list_kernel(near_ref, count_ref, out_ref):
    place = place_of()
    source = source_of(near_ref[...], place, LEAF)
    count = count_ref[...]
    leaf = lax.broadcasted_iota(jnp.int32, (1, LEAF), 1)
    own_at = jnp.zeros((1, LEAF), jnp.int32)
    rest_at = jnp.zeros((1, LEAF), jnp.int32)
    own = [jnp.full((1, LEAF), LEAF, jnp.int32) for _ in range(SLOTS - 1)]
    places = []
    for k in range(1, NEAR):
        src = source[k:k + 1]
        live = count > k
        here = jnp.logical_and(jnp.logical_and(src < LEAF, live), own_at < SLOTS - 1)
        for s in range(SLOTS - 1):
            own[s] = jnp.where(jnp.logical_and(here, own_at == s), src, own[s])
        own_at = own_at + jnp.where(here, 1, 0)
        rest = jnp.logical_and(live, jnp.logical_not(here))
        places.append((rest, rest_at))
        rest_at = rest_at + jnp.where(rest, 1, 0)
    row = lax.broadcasted_iota(jnp.int32, (LEAF, LEAF), 0)
    col = lax.broadcasted_iota(jnp.int32, (LEAF, LEAF), 1)
    before = jnp.where(row < col, 1.0, 0.0).astype(bf16)
    counts = jnp.broadcast_to(rest_at.astype(f32), (16, LEAF)).astype(bf16)
    base = dot(counts, before)[0:1]
    at = [jnp.where(rest, base + pos.astype(f32), -1.0) for rest, pos in places]
    values = jnp.concatenate(at + [source[k:k + 1].astype(f32) for k in range(1, NEAR)], axis=0).astype(bf16)
    columns = dot(jnp.where(row == col, 1.0, 0.0).astype(bf16), values, NT)
    lanes = lax.broadcasted_iota(jnp.int32, (LEAF, PTS), 1).astype(f32)
    word = lax.broadcasted_iota(jnp.int32, (LEAF, 1), 0).astype(f32) * 128.0
    flat = jnp.zeros((LEAF, PTS), f32)
    for k in range(NEAR - 1):
        flat = flat + jnp.where(columns[:, k:k + 1] == lanes, word + columns[:, NEAR - 1 + k:NEAR + k], 0.0)
    flat = jnp.sum(flat, axis=0, keepdims=True)
    total = jnp.sum(rest_at.astype(f32), axis=1, keepdims=True)
    flat = jnp.where(lanes[0:1] < total, flat, LEAF * 128.0)
    out_ref[...] = jnp.zeros((16, PTS), jnp.int32)
    out_ref[0:1, 0:LEAF] = leaf
    for s in range(SLOTS - 1):
        out_ref[s + 1:s + 2, 0:LEAF] = own[s]
    out_ref[REST_ROW:REST_ROW + 1, :] = flat.astype(jnp.int32)
    out_ref[COUNT_ROW:COUNT_ROW + 1, :] = jnp.broadcast_to(total, (1, PTS)).astype(jnp.int32)


def upward(coords_ref, x_ref, basis_ref, t1_ref, t2_ref, pack_ref):
    tiles = []
    for t in range(LEAF // 2):
        xa = x_ref[:, t * 512:t * 512 + 256]
        xb = x_ref[:, t * 512 + 256:t * 512 + 512]
        ra, rb = fold(dot(stacked_split(xa, xb), wide_split(basis_ref[:, t * 128:t * 128 + 128])))
        q = jnp.where(lanes_low(ra.shape), ra, rb)
        pack_ref[t] = q
        tiles.append(q)
    mids = []
    parts = []
    for m in range(MID):
        a0, b0 = halves(tiles[2 * m])
        a1, b1 = halves(tiles[2 * m + 1])
        e0 = t1_ref[:, m * 256:m * 256 + 128]
        e1 = t1_ref[:, m * 256 + 128:m * 256 + 256]
        lhs = stacked_split(jnp.concatenate([a0, a1], axis=1), jnp.concatenate([b0, b1], axis=1))
        parts.append(fold(dot(lhs, wide_split(jnp.concatenate([e0, e0, e1, e1], axis=0)))))
    for t in range(MID // 2):
        (top0, bot0), (top1, bot1) = parts[2 * t], parts[2 * t + 1]
        low = lanes_low(top0.shape)
        mid = jnp.where(low, top0, bot1) + swap_halves(jnp.where(low, top1, bot0))
        pack_ref[LEAF // 2 + t] = mid
        mids.append(mid)
    both = [halves(m) for m in mids]
    weights = [t2_ref[:, t * 128:t * 128 + 128] for t in range(MID // 2)]
    lhs = stacked_split(
        jnp.concatenate([b[0] for b in both], axis=1), jnp.concatenate([b[1] for b in both], axis=1)
    )
    top, bot = fold(dot(lhs, wide_split(jnp.concatenate([w for w in weights for _ in range(2)], axis=0))))
    for i in range(2 * LEAF):
        for c in range(3):
            pack_ref[15 + c, i:i + 1, :] = coords_ref[c:c + 1, i * 128:i * 128 + 128]
    zero = jnp.zeros((16, 128), f32)
    for c in range(3):
        pack_ref[15 + c, 48:64, :] = zero
    s = jnp.where(lanes_low(top.shape), top, bot)
    return s + swap_halves(s)


def leaf_rows(pack_ref, leaf):
    row = lax.broadcasted_iota(jnp.int32, (8, PTS), 0)
    out = jnp.zeros((8, PTS), f32)
    for c in range(3):
        line = jnp.concatenate(
            [pack_ref[15 + c, 2 * leaf:2 * leaf + 1, :], pack_ref[15 + c, 2 * leaf + 1:2 * leaf + 2, :]], axis=1
        )
        out = jnp.where(row == c, line, out)
    return out


def pieces(a):
    h = a.astype(bf16).astype(f32)
    r = a - h
    m = r.astype(bf16).astype(f32)
    return h, m, r - m


def identity():
    return jnp.where(
        lax.broadcasted_iota(jnp.int32, (PTS, PTS), 0) == lax.broadcasted_iota(jnp.int32, (PTS, PTS), 1), 1.0, 0.0
    ).astype(bf16)


def prepare(pack_ref, x_ref, leaf, at, eye, centres, feats, xs):
    row = lax.broadcasted_iota(jnp.int32, (8, PTS), 0)
    source = leaf_rows(pack_ref, leaf)
    centre = jnp.broadcast_to(jnp.sum(source, axis=1, keepdims=True) * (1.0 / PTS), (8, PTS))
    centres[at] = centre
    d = source - centre
    sq = jnp.sum(d * d, axis=0, keepdims=True) + smooth_sq
    h, m, l = pieces(jnp.where(row < 3, -2.0 * d, jnp.where(row == 3, 1.0, jnp.where(row == 4, sq, 0.0))))
    rows = jnp.concatenate([h, m, h, l, m, h, jnp.zeros((80, PTS), f32)], axis=0).astype(bf16)
    feats[at] = dot(eye, rows, NT).astype(bf16)
    xh, xl = split(x_ref[:, leaf * PTS:leaf * PTS + PTS] * inv_four_pi)
    xs[at] = jnp.concatenate([xh, xl], axis=0)


def pairs(ls, js, targets, centres, feats, xs, acc):
    unit = jnp.where(lax.broadcasted_iota(jnp.int32, (8, PTS), 0) == 4, 1.0, 0.0)
    row = lax.broadcasted_iota(jnp.int32, (8, PTS), 0)
    dist = []
    for l, j in zip(ls, js):
        d = targets[l] - centres[j]
        sq = jnp.sum(d * d, axis=0, keepdims=True)
        h, m, low = pieces(jnp.where(row == 3, sq, d + unit))
        rows = jnp.concatenate([h, h, m, h, m, low], axis=0).astype(bf16)
        dist.append(dot(feats[j][:, :48], rows))
    for l, j, d2 in zip(ls, js, dist):
        kh, kl = split(lax.rsqrt(d2))
        x = xs[j]
        r = dot(x, kh) + dot(x, kl)
        acc[l] += r[:64] + r[64:]


def place_tile(tile, low_ref, high_ref, at):
    other = swap_halves(tile)
    low = lanes_low(tile.shape)
    for i, (here, there) in enumerate(((tile, other), (other, tile))):
        h, l = split(jnp.where(low, here, 0.0))
        low_ref[at + i] = jnp.concatenate([h, l], axis=0)
        h, l = split(jnp.where(low, 0.0, there))
        high_ref[at + i] = jnp.concatenate([h, l], axis=0)


def coupled(sources, weights, low_ref, high_ref):
    lhs = jnp.concatenate(
        [
            jnp.concatenate([low_ref[row[f]] + high_ref[row[f + 1]] for f in range(0, len(row), 2)], axis=1)
            for row in sources
        ],
        axis=0,
    )
    out = dot(lhs, wide_split(jnp.concatenate(weights, axis=0)))
    s = out[:, :128] + out[:, 128:]
    even, odd = s[0:64] + s[64:128], s[128:192] + s[192:256]
    return jnp.where(lanes_low(even.shape), even, odd)


def top_coupled(picks, c2_ref):
    tiles = []
    for f in range(0, FAR2, 2):
        a = jnp.concatenate([picks[f], swap_halves(picks[f])], axis=0)
        b = jnp.concatenate([swap_halves(picks[f + 1]), picks[f + 1]], axis=0)
        tiles.append(jnp.where(lanes_low(a.shape), a, b))
    th, tl = split(jnp.concatenate(tiles, axis=1))
    w = jnp.concatenate([c2_ref[f] for f in range(FAR2)], axis=0)
    wh, wl = split(jnp.concatenate([w, w], axis=1))
    y2 = dot(th, wh) + dot(tl, wh) + dot(th, wl)
    return jnp.where(lanes_low((32, 128)), y2[:32], y2[32:])


def main_kernel(
    list_ref, far0_ref, far1_ref, far2_ref, coords_hbm, x_hbm, basis_hbm, t1_hbm, t2_hbm, c0_hbm, c1_hbm, c2_hbm,
    acc_out, pack_out, p2_ref, x2_ref, centres_out, feats_out, xs_out,
    coords, x, x1, basis, t1, t2, c0, c1, c2, pack, p1, p2, acc, targets, centres, feats, xs,
    part, parts, y2_part, y2_parts, y1, y1_part, y0, q_low, q_high, m_low, m_high,
    load_sem, part_send, part_recv, y2_send, y2_recv, swap_send, swap_recv, out_sem,
):
    group = lax.axis_index("grp")
    lane = lax.axis_index("lane")
    place = group * LANES + lane
    even = lax.rem(lane, 2) == 0
    partner = (group, lane + 1 - 2 * lax.rem(lane, 2))
    beyond = lax.rem(place + jnp.where(even, DEVS - 1, 1), DEVS)
    beyond = (beyond // LANES, lax.rem(beyond, LANES))

    barrier = pltpu.get_barrier_semaphore()
    for d in range(1, LANES):
        pl.semaphore_signal(barrier, inc=1, device_id=(group, lax.rem(lane + d, LANES)), device_id_type=MESH)
    for d in range(1, GROUPS):
        pl.semaphore_signal(barrier, inc=1, device_id=(lax.rem(group + d, GROUPS), lane), device_id_type=MESH)
    pl.semaphore_signal(barrier, inc=1, device_id=beyond, device_id_type=MESH)

    loads = [
        pltpu.make_async_copy(src, dst, load_sem.at[i])
        for i, (src, dst) in enumerate(
            [(x_hbm.at[:, c * 1536:c * 1536 + 1536], x.at[:, c * 1536:c * 1536 + 1536]) for c in range(4)]
            + [(basis_hbm.at[r * 64:r * 64 + 64], basis.at[r * 64:r * 64 + 64]) for r in range(4)]
            + [(t1_hbm, t1), (t2_hbm, t2), (coords_hbm, coords)]
            + [(c0_hbm.at[r * 2:r * 2 + 2], c0.at[r * 2:r * 2 + 2]) for r in range(4)]
            + [(c1_hbm, c1), (c2_hbm, c2)]
        )
    ]
    for c in loads:
        c.start()
    for c in loads[:11]:
        c.wait()
    top = upward(coords, x, basis, t1, t2, pack)
    part[...] = jnp.where(lanes_low((32, 128)), top[:32], top[32:])
    pl.semaphore_wait(barrier, LANES + GROUPS - 1)

    def part_copy(d):
        peer = lax.rem(group + d, GROUPS)
        return (
            pltpu.make_async_remote_copy(
                part, parts.at[group], part_send.at[d], part_recv.at[group], (peer, lane), MESH
            ),
            pltpu.make_async_remote_copy(
                part, parts.at[peer], part_send.at[d], part_recv.at[peer], (peer, lane), MESH
            ),
        )

    def y2_copy(d):
        peer = lax.rem(lane + d, LANES)
        return (
            pltpu.make_async_remote_copy(
                y2_part, y2_parts.at[lane], y2_send.at[d], y2_recv.at[lane], (group, peer), MESH
            ),
            pltpu.make_async_remote_copy(
                y2_part, y2_parts.at[peer], y2_send.at[d], y2_recv.at[peer], (group, peer), MESH
            ),
        )

    def swap(src, dst, i, device):
        return pltpu.make_async_remote_copy(src, dst, swap_send.at[i], swap_recv.at[i], device, MESH)

    swaps = [
        swap(pack, p2, 0, beyond),
        swap(pack, p1, 1, partner),
        swap(x, x1, 2, partner),
        swap(x, x2_ref, 3, beyond),
    ]
    for d in range(1, GROUPS):
        part_copy(d)[0].start()
    for c in swaps:
        c.start()

    eye = identity()
    for leaf in range(LEAF):
        targets[leaf] = leaf_rows(pack, leaf)
        prepare(pack, x, leaf, leaf, eye, centres, feats, xs)
        acc[leaf] = jnp.zeros((64, PTS), f32)
    centres[2 * LEAF] = jnp.zeros((8, PTS), f32)
    feats[2 * LEAF] = feats[0]
    xs[2 * LEAF] = jnp.zeros((128, PTS), bf16)

    def leaves(i, _):
        at = [STEP * i + u for u in range(STEP) for s in range(SLOTS)]
        js = [list_ref[s, STEP * i + u] for u in range(STEP) for s in range(SLOTS)]
        pairs(at, [jnp.where(j == LEAF, 2 * LEAF, j) for j in js], targets, centres, feats, xs, acc)
        return 0

    lax.fori_loop(0, 2, leaves, 0)

    for c in loads[11:]:
        c.wait()
    for d in range(1, GROUPS):
        part_copy(d)[1].wait_recv()
    parts[group] = part[...]
    mine = top_coupled([parts[far2_ref[f, group]] for f in range(FAR2)], c2)
    y2_part[...] = mine
    y2_parts[lane] = mine
    for d in range(1, LANES):
        y2_copy(d)[0].start()

    lax.fori_loop(2, LEAF // STEP, leaves, 0)

    for c in swaps[:2]:
        c.wait()
    for b, p in enumerate((pack, p1, p2)):
        for t in range(LEAF // 2):
            place_tile(p[t], q_low, q_high, LEAF * b + 2 * t)
        for t in range(MID // 2):
            place_tile(p[LEAF // 2 + t], m_low, m_high, MID * b + 2 * t)
    for t in range(MID // 2):
        at = slice(t * 128, t * 128 + 128)
        y1_part[t] = coupled(
            [[source_of(far1_ref[f, 2 * t + i], place, MID) for f in range(FAR1)] for i in range(2)],
            [c1[f, :, at] for f in range(FAR1)], m_low, m_high,
        )

    def across(m, _):
        for u in range(2):
            t = 2 * m + u
            at = pl.ds(pl.multiple_of(t * 128, 128), 128)
            y0[t] = coupled(
                [[source_of(far0_ref[f, 2 * t + i], place, LEAF) for f in range(FAR0)] for i in range(2)],
                [c0[f, :, at] for f in range(FAR0)], q_low, q_high,
            )
        return 0

    lax.fori_loop(0, MID, across, 0)

    swaps[2].wait()
    for leaf in range(LEAF):
        prepare(p1, x1, leaf, LEAF + leaf, eye, centres, feats, xs)
    outs = [
        pltpu.make_async_copy(src, dst, out_sem.at[i])
        for i, (src, dst) in enumerate(
            [
                (pack, pack_out), (p2, p2_ref), (centres.at[0:48], centres_out),
                (feats.at[0:24], feats_out.at[0:24]), (feats.at[24:48], feats_out.at[24:48]),
                (xs.at[0:24], xs_out.at[0:24]), (xs.at[24:48], xs_out.at[24:48]),
                (acc, acc_out),
            ]
        )
    ]
    for c in outs[:-1]:
        c.start()

    for d in range(1, LANES):
        y2_copy(d)[1].wait_recv()
    y2 = y2_parts[0]
    for r in range(1, LANES):
        y2 = y2 + y2_parts[r]
    other = swap_halves(y2)
    low = lanes_low(y2.shape)
    y2 = jnp.concatenate([jnp.where(low, y2, other), jnp.where(low, other, y2)], axis=0)
    for t in range(MID // 2):
        w = t2[:, t * 128:t * 128 + 128]
        one, two = transposed(*halves(y2), jnp.concatenate([w, w], axis=0))
        y = y1_part[t] + jnp.where(lanes_low(one.shape), one, two)
        other = swap_halves(y)
        low = lanes_low(y.shape)
        y1[2 * t] = jnp.where(low, y, other)
        y1[2 * t + 1] = jnp.where(low, other, y)

    for m in range(MID):
        for u in range(2):
            t = 2 * m + u
            at = slice(t * 128, t * 128 + 128)
            w = t1[:, at]
            one, two = transposed(*halves(y1[m]), jnp.concatenate([w, w], axis=0))
            y = y0[t] + jnp.where(lanes_low(one.shape), one, two)
            one, two = transposed(*halves(y), basis[:, at])
            acc[2 * t] += one
            acc[2 * t + 1] += two
    outs[-1].start()
    for d in range(1, GROUPS):
        part_copy(d)[0].wait_send()
    for d in range(1, LANES):
        y2_copy(d)[0].wait_send()

    swaps[3].wait()
    for c in outs:
        c.wait()


def rest_kernel(
    list_ref, own_hbm, p2_hbm, x2_hbm, acc_hbm, centres_hbm, feats_hbm, xs_hbm, out_ref,
    own, p2, targets, centres, feats, xs, acc, x, sem, out_sem,
):
    moves = [
        pltpu.make_async_copy(src, dst, sem.at[i])
        for i, (src, dst) in enumerate(
            [(own_hbm, own), (p2_hbm, p2)]
            + [(x2_hbm.at[:, c * 1536:c * 1536 + 1536], x.at[:, c * 1536:c * 1536 + 1536]) for c in range(4)]
            + [
                (acc_hbm, acc.at[0:24]), (centres_hbm, centres.at[0:48]),
                (feats_hbm.at[0:24], feats.at[0:24]), (feats_hbm.at[24:48], feats.at[24:48]),
                (xs_hbm.at[0:24], xs.at[0:24]), (xs_hbm.at[24:48], xs.at[24:48]),
            ]
        )
    ]
    for c in moves:
        c.start()
    targets[LEAF] = jnp.zeros((8, PTS), f32)
    acc[LEAF] = jnp.zeros((64, PTS), f32)
    eye = identity()
    for c in moves[:6]:
        c.wait()
    for leaf in range(LEAF):
        targets[leaf] = leaf_rows(own, leaf)
        prepare(p2, x, leaf, 2 * LEAF + leaf, eye, centres, feats, xs)
    for c in moves[6:]:
        c.wait()

    @pl.loop(0, (list_ref[COUNT_ROW, 0] + (UNROLL - 1)) // UNROLL)
    def _(i):
        words = [list_ref[REST_ROW, i * UNROLL + u] for u in range(UNROLL)]
        pairs(
            [lax.shift_right_logical(w, 7) for w in words], [w & 127 for w in words], targets, centres, feats, xs, acc
        )

    outs = [
        pltpu.make_async_copy(acc.at[leaf], out_ref.at[:, leaf * PTS:leaf * PTS + PTS], out_sem.at[leaf])
        for leaf in range(LEAF)
    ]
    for c in outs:
        c.start()
    for c in outs:
        c.wait()


VM = pl.BlockSpec(memory_space=pltpu.VMEM)
SM = pl.BlockSpec(memory_space=pltpu.SMEM)
ANY = pl.BlockSpec(memory_space=pl.ANY)
DMA = pltpu.SemaphoreType.DMA


def params(mib, **more):
    return pltpu.CompilerParams(vmem_limit_bytes=mib << 20, **more)


def cost(size):
    return pl.CostEstimate(flops=size, bytes_accessed=1000, transcendentals=0)


def shape(*dims, dtype=f32):
    return jax.ShapeDtypeStruct(dims, dtype)


def local(
    coords, charges, basis, transfer1, transfer2, coupling0, coupling1, coupling2, near_list, near_count, far0_list,
    far1_list, far2_list,
):
    lists = pl.pallas_call(
        list_kernel, out_shape=shape(16, PTS, dtype=jnp.int32), in_specs=[VM, VM], out_specs=VM,
        compiler_params=params(56), cost_estimate=cost(1000), name="lists",
    )(near_list.T, near_count.reshape(1, LEAF))
    wide = LEAF * PTS
    acc, pack, p2, x2, centres, feats, xs = pl.pallas_call(
        main_kernel,
        out_shape=(
            shape(LEAF, 64, PTS), shape(18, 64, 128), shape(18, 64, 128), shape(64, wide), shape(2 * LEAF, 8, PTS),
            shape(2 * LEAF, PTS, 128, dtype=bf16), shape(2 * LEAF, 128, PTS, dtype=bf16),
        ),
        in_specs=[SM] * 4 + [ANY] * 8,
        out_specs=(ANY,) * 7,
        scratch_shapes=[
            pltpu.VMEM((3, wide), f32), pltpu.VMEM((64, wide), f32), pltpu.VMEM((64, wide), f32),
            pltpu.VMEM((PTS, LEAF * RANK), f32), pltpu.VMEM((RANK, LEAF * RANK), f32),
            pltpu.VMEM((RANK, MID * RANK), f32), pltpu.VMEM((FAR0, RANK, LEAF * RANK), f32),
            pltpu.VMEM((FAR1, RANK, MID * RANK), f32), pltpu.VMEM((FAR2, RANK, RANK), f32),
            pltpu.VMEM((18, 64, 128), f32), pltpu.VMEM((18, 64, 128), f32), pltpu.VMEM((18, 64, 128), f32),
            pltpu.VMEM((LEAF, 64, PTS), f32), pltpu.VMEM((LEAF, 8, PTS), f32),
            pltpu.VMEM((2 * LEAF + 1, 8, PTS), f32), pltpu.VMEM((2 * LEAF + 1, PTS, 128), bf16),
            pltpu.VMEM((2 * LEAF + 1, 128, PTS), bf16),
            pltpu.VMEM((32, 128), f32), pltpu.VMEM((GROUPS, 32, 128), f32), pltpu.VMEM((32, 128), f32),
            pltpu.VMEM((LANES, 32, 128), f32), pltpu.VMEM((MID, 64, 128), f32),
            pltpu.VMEM((MID // 2, 64, 128), f32), pltpu.VMEM((LEAF // 2, 64, 128), f32),
            pltpu.VMEM((3 * LEAF, 128, 128), bf16), pltpu.VMEM((3 * LEAF, 128, 128), bf16),
            pltpu.VMEM((3 * MID, 128, 128), bf16), pltpu.VMEM((3 * MID, 128, 128), bf16),
            DMA((17,)), DMA((GROUPS,)), DMA((GROUPS,)), DMA((LANES,)), DMA((LANES,)), DMA((4,)), DMA((4,)),
            DMA((8,)),
        ],
        compiler_params=params(56, collective_id=0, has_side_effects=True),
        cost_estimate=cost(1000),
        name="main",
    )(
        lists, far0_list.T, far1_list.T, far2_list.T, coords, charges, basis, transfer1, transfer2, coupling0,
        coupling1, coupling2,
    )
    return pl.pallas_call(
        rest_kernel,
        out_shape=shape(64, wide),
        in_specs=[SM] + [ANY] * 7,
        out_specs=ANY,
        scratch_shapes=[
            pltpu.VMEM((18, 64, 128), f32), pltpu.VMEM((18, 64, 128), f32), pltpu.VMEM((LEAF + 1, 8, PTS), f32),
            pltpu.VMEM((3 * LEAF, 8, PTS), f32), pltpu.VMEM((3 * LEAF, PTS, 128), bf16),
            pltpu.VMEM((3 * LEAF, 128, PTS), bf16), pltpu.VMEM((LEAF + 1, 64, PTS), f32), pltpu.VMEM((64, wide), f32),
            DMA((12,)), DMA((LEAF,)),
        ],
        compiler_params=params(56),
        cost_estimate=cost(1000),
        name="rest",
    )(lists, pack, p2, x2, acc, centres, feats, xs)


def solution(mesh):
    placed = (
        P(None, AXES),
        P(None, AXES),
        P(None, AXES),
        P(None, AXES),
        P(None, AXES),
        P(None, None, AXES),
        P(None, None, AXES),
        P(None, None, "grp"),
        P(AXES, None),
        P(AXES),
        P(AXES, None),
        P(AXES, None),
        P(),
    )
    return jax.shard_map(local, mesh=mesh, in_specs=placed, out_specs=P(None, AXES), check_vma=False)
```

```python
import math

import jax
import jax.numpy as jnp
from jax import lax
from jax.experimental import pallas as pl
from jax.experimental.pallas import tpu as pltpu
from jax.sharding import PartitionSpec as P

AXES = ("grp", "lane")
LANES = 8
DEVS = 128
LEAF = 24
MID = 6
PTS = 256
RANK = 64
NEAR = 9
FAR0 = 8
FAR1 = 4
FAR2 = 4
UNROLL = 24
SLOTS = 5
REST_ROW = 8
COUNT_ROW = 9
STEP = 6
GROUPS = 16
MESH = pl.DeviceIdType.MESH
inv_four_pi = 1.0 / (4.0 * math.pi)
smooth_sq = 5e-05
bf16 = jnp.bfloat16
f32 = jnp.float32
NT = (((1,), (1,)), ((), ()))


def dot(a, b, dims=(((1,), (0,)), ((), ()))):
    return lax.dot_general(a, b, dims, preferred_element_type=f32)


def split(a):
    high = a.astype(bf16)
    return high, (a - high.astype(f32)).astype(bf16)


def lanes_low(shape):
    return lax.broadcasted_iota(jnp.int32, shape, len(shape) - 1) < RANK


def swap_halves(a):
    return pltpu.roll(a, RANK, 1)


def halves(tile):
    low = lanes_low(tile.shape)
    return jnp.where(low, tile, 0.0), jnp.where(low, 0.0, tile)


def place_of():
    return lax.axis_index("grp") * LANES + lax.axis_index("lane")


def source_of(entry, place, width):
    even = lax.rem(place, 2) == 0
    rel = entry - place * width
    rel = jnp.where(rel < -width, rel + DEVS * width, jnp.where(rel >= 2 * width, rel - DEVS * width, rel))
    low_off = jnp.where(even, 3 * width, 2 * width)
    high_off = jnp.where(even, 0, width)
    source = rel + jnp.where(rel < 0, low_off, jnp.where(rel >= width, high_off, 0))
    return jnp.minimum(jnp.maximum(source, 0), 3 * width - 1)


def stacked_split(rows_a, rows_b):
    ah, al = split(rows_a)
    bh, bl = split(rows_b)
    return jnp.concatenate([ah, bh, al, bl], axis=0)


def wide_split(a):
    h, l = split(a)
    return jnp.concatenate([h, l], axis=1)


def fold(out):
    s = out[:, :128] + out[:, 128:]
    return s[0:64] + s[128:192], s[64:128] + s[192:256]


def transposed(rows_a, rows_b, weights):
    lhs = stacked_split(rows_a, rows_b)
    wh, wl = split(weights)
    r = dot(lhs, wh, NT)
    r2 = dot(lhs[:128], wl, NT)
    return r[0:64] + r[128:192] + r2[0:64], r[64:128] + r[192:256] + r2[64:128]


def list_kernel(near_ref, count_ref, out_ref):
    place = place_of()
    source = source_of(near_ref[...], place, LEAF)
    count = count_ref[...]
    leaf = lax.broadcasted_iota(jnp.int32, (1, LEAF), 1)
    own_at = jnp.zeros((1, LEAF), jnp.int32)
    rest_at = jnp.zeros((1, LEAF), jnp.int32)
    own = [jnp.full((1, LEAF), LEAF, jnp.int32) for _ in range(SLOTS - 1)]
    places = []
    for k in range(1, NEAR):
        src = source[k:k + 1]
        live = count > k
        here = jnp.logical_and(jnp.logical_and(src < LEAF, live), own_at < SLOTS - 1)
        for s in range(SLOTS - 1):
            own[s] = jnp.where(jnp.logical_and(here, own_at == s), src, own[s])
        own_at = own_at + jnp.where(here, 1, 0)
        rest = jnp.logical_and(live, jnp.logical_not(here))
        places.append((rest, rest_at))
        rest_at = rest_at + jnp.where(rest, 1, 0)
    row = lax.broadcasted_iota(jnp.int32, (LEAF, LEAF), 0)
    col = lax.broadcasted_iota(jnp.int32, (LEAF, LEAF), 1)
    before = jnp.where(row < col, 1.0, 0.0).astype(bf16)
    counts = jnp.broadcast_to(rest_at.astype(f32), (16, LEAF)).astype(bf16)
    base = dot(counts, before)[0:1]
    at = [jnp.where(rest, base + pos.astype(f32), -1.0) for rest, pos in places]
    values = jnp.concatenate(at + [source[k:k + 1].astype(f32) for k in range(1, NEAR)], axis=0).astype(bf16)
    columns = dot(jnp.where(row == col, 1.0, 0.0).astype(bf16), values, NT)
    lanes = lax.broadcasted_iota(jnp.int32, (LEAF, PTS), 1).astype(f32)
    word = lax.broadcasted_iota(jnp.int32, (LEAF, 1), 0).astype(f32) * 128.0
    flat = jnp.zeros((LEAF, PTS), f32)
    for k in range(NEAR - 1):
        flat = flat + jnp.where(columns[:, k:k + 1] == lanes, word + columns[:, NEAR - 1 + k:NEAR + k], 0.0)
    flat = jnp.sum(flat, axis=0, keepdims=True)
    total = jnp.sum(rest_at.astype(f32), axis=1, keepdims=True)
    flat = jnp.where(lanes[0:1] < total, flat, LEAF * 128.0)
    out_ref[...] = jnp.zeros((16, PTS), jnp.int32)
    out_ref[0:1, 0:LEAF] = leaf
    for s in range(SLOTS - 1):
        out_ref[s + 1:s + 2, 0:LEAF] = own[s]
    out_ref[REST_ROW:REST_ROW + 1, :] = flat.astype(jnp.int32)
    out_ref[COUNT_ROW:COUNT_ROW + 1, :] = jnp.broadcast_to(total, (1, PTS)).astype(jnp.int32)


def upward(coords_ref, x_ref, basis_ref, t1_ref, t2_ref, pack_ref):
    tiles = []
    for t in range(LEAF // 2):
        xa = x_ref[:, t * 512:t * 512 + 256]
        xb = x_ref[:, t * 512 + 256:t * 512 + 512]
        ra, rb = fold(dot(stacked_split(xa, xb), wide_split(basis_ref[:, t * 128:t * 128 + 128])))
        q = jnp.where(lanes_low(ra.shape), ra, rb)
        pack_ref[t] = q
        tiles.append(q)
    mids = []
    parts = []
    for m in range(MID):
        a0, b0 = halves(tiles[2 * m])
        a1, b1 = halves(tiles[2 * m + 1])
        e0 = t1_ref[:, m * 256:m * 256 + 128]
        e1 = t1_ref[:, m * 256 + 128:m * 256 + 256]
        lhs = stacked_split(jnp.concatenate([a0, a1], axis=1), jnp.concatenate([b0, b1], axis=1))
        parts.append(fold(dot(lhs, wide_split(jnp.concatenate([e0, e0, e1, e1], axis=0)))))
    for t in range(MID // 2):
        (top0, bot0), (top1, bot1) = parts[2 * t], parts[2 * t + 1]
        low = lanes_low(top0.shape)
        mid = jnp.where(low, top0, bot1) + swap_halves(jnp.where(low, top1, bot0))
        pack_ref[LEAF // 2 + t] = mid
        mids.append(mid)
    both = [halves(m) for m in mids]
    weights = [t2_ref[:, t * 128:t * 128 + 128] for t in range(MID // 2)]
    lhs = stacked_split(
        jnp.concatenate([b[0] for b in both], axis=1), jnp.concatenate([b[1] for b in both], axis=1)
    )
    top, bot = fold(dot(lhs, wide_split(jnp.concatenate([w for w in weights for _ in range(2)], axis=0))))
    for i in range(2 * LEAF):
        for c in range(3):
            pack_ref[15 + c, i:i + 1, :] = coords_ref[c:c + 1, i * 128:i * 128 + 128]
    zero = jnp.zeros((16, 128), f32)
    for c in range(3):
        pack_ref[15 + c, 48:64, :] = zero
    s = jnp.where(lanes_low(top.shape), top, bot)
    return s + swap_halves(s)


def leaf_rows(pack_ref, leaf):
    row = lax.broadcasted_iota(jnp.int32, (8, PTS), 0)
    out = jnp.zeros((8, PTS), f32)
    for c in range(3):
        line = jnp.concatenate(
            [pack_ref[15 + c, 2 * leaf:2 * leaf + 1, :], pack_ref[15 + c, 2 * leaf + 1:2 * leaf + 2, :]], axis=1
        )
        out = jnp.where(row == c, line, out)
    return out


def pieces(a):
    h = a.astype(bf16).astype(f32)
    r = a - h
    m = r.astype(bf16).astype(f32)
    return h, m, r - m


def identity():
    return jnp.where(
        lax.broadcasted_iota(jnp.int32, (PTS, PTS), 0) == lax.broadcasted_iota(jnp.int32, (PTS, PTS), 1), 1.0, 0.0
    ).astype(bf16)


def prepare(pack_ref, x_ref, leaf, at, eye, centres, feats, xs):
    row = lax.broadcasted_iota(jnp.int32, (8, PTS), 0)
    source = leaf_rows(pack_ref, leaf)
    centre = jnp.broadcast_to(jnp.sum(source, axis=1, keepdims=True) * (1.0 / PTS), (8, PTS))
    centres[at] = centre
    d = source - centre
    sq = jnp.sum(d * d, axis=0, keepdims=True) + smooth_sq
    h, m, l = pieces(jnp.where(row < 3, -2.0 * d, jnp.where(row == 3, 1.0, jnp.where(row == 4, sq, 0.0))))
    rows = jnp.concatenate([h, m, h, l, m, h, jnp.zeros((80, PTS), f32)], axis=0).astype(bf16)
    feats[at] = dot(eye, rows, NT).astype(bf16)
    xh, xl = split(x_ref[:, leaf * PTS:leaf * PTS + PTS] * inv_four_pi)
    xs[at] = jnp.concatenate([xh, xl], axis=0)


def pairs(ls, js, targets, centres, feats, xs, acc):
    unit = jnp.where(lax.broadcasted_iota(jnp.int32, (8, PTS), 0) == 4, 1.0, 0.0)
    row = lax.broadcasted_iota(jnp.int32, (8, PTS), 0)
    dist = []
    for l, j in zip(ls, js):
        d = targets[l] - centres[j]
        sq = jnp.sum(d * d, axis=0, keepdims=True)
        h, m, low = pieces(jnp.where(row == 3, sq, d + unit))
        rows = jnp.concatenate([h, h, m, h, m, low], axis=0).astype(bf16)
        dist.append(dot(feats[j][:, :48], rows))
    for l, j, d2 in zip(ls, js, dist):
        kh, kl = split(lax.rsqrt(d2))
        x = xs[j]
        r = dot(x, kh) + dot(x, kl)
        acc[l] += r[:64] + r[64:]


def place_tile(tile, low_ref, high_ref, at):
    other = swap_halves(tile)
    low = lanes_low(tile.shape)
    for i, (here, there) in enumerate(((tile, other), (other, tile))):
        h, l = split(jnp.where(low, here, 0.0))
        low_ref[at + i] = jnp.concatenate([h, l], axis=0)
        h, l = split(jnp.where(low, 0.0, there))
        high_ref[at + i] = jnp.concatenate([h, l], axis=0)


def coupled(sources, weights, low_ref, high_ref):
    lhs = jnp.concatenate(
        [
            jnp.concatenate([low_ref[row[f]] + high_ref[row[f + 1]] for f in range(0, len(row), 2)], axis=1)
            for row in sources
        ],
        axis=0,
    )
    out = dot(lhs, wide_split(jnp.concatenate(weights, axis=0)))
    s = out[:, :128] + out[:, 128:]
    even, odd = s[0:64] + s[64:128], s[128:192] + s[192:256]
    return jnp.where(lanes_low(even.shape), even, odd)


def top_coupled(picks, c2_ref):
    tiles = []
    for f in range(0, FAR2, 2):
        a = jnp.concatenate([picks[f], swap_halves(picks[f])], axis=0)
        b = jnp.concatenate([swap_halves(picks[f + 1]), picks[f + 1]], axis=0)
        tiles.append(jnp.where(lanes_low(a.shape), a, b))
    th, tl = split(jnp.concatenate(tiles, axis=1))
    w = jnp.concatenate([c2_ref[f] for f in range(FAR2)], axis=0)
    wh, wl = split(jnp.concatenate([w, w], axis=1))
    y2 = dot(th, wh) + dot(tl, wh) + dot(th, wl)
    return jnp.where(lanes_low((32, 128)), y2[:32], y2[32:])


def main_kernel(
    list_ref, far0_ref, far1_ref, far2_ref, coords_hbm, x_hbm, basis_hbm, t1_hbm, t2_hbm, c0_hbm, c1_hbm, c2_hbm,
    acc_out, pack_out, p2_ref, x2_ref, centres_out, feats_out, xs_out,
    coords, x, x1, basis, t1, t2, c0, c1, c2, pack, p1, p2, acc, targets, centres, feats, xs,
    part, parts, y2_part, y2_parts, y1, y1_part, y0, q_low, q_high, m_low, m_high,
    load_sem, part_send, part_recv, y2_send, y2_recv, swap_send, swap_recv, out_sem,
):
    group = lax.axis_index("grp")
    lane = lax.axis_index("lane")
    place = group * LANES + lane
    even = lax.rem(lane, 2) == 0
    partner = (group, lane + 1 - 2 * lax.rem(lane, 2))
    beyond = lax.rem(place + jnp.where(even, DEVS - 1, 1), DEVS)
    beyond = (beyond // LANES, lax.rem(beyond, LANES))

    barrier = pltpu.get_barrier_semaphore()
    for d in range(1, LANES):
        pl.semaphore_signal(barrier, inc=1, device_id=(group, lax.rem(lane + d, LANES)), device_id_type=MESH)
    for d in range(1, GROUPS):
        pl.semaphore_signal(barrier, inc=1, device_id=(lax.rem(group + d, GROUPS), lane), device_id_type=MESH)
    pl.semaphore_signal(barrier, inc=1, device_id=beyond, device_id_type=MESH)

    loads = [
        pltpu.make_async_copy(src, dst, load_sem.at[i])
        for i, (src, dst) in enumerate(
            [(x_hbm.at[:, c * 1536:c * 1536 + 1536], x.at[:, c * 1536:c * 1536 + 1536]) for c in range(4)]
            + [(basis_hbm.at[r * 64:r * 64 + 64], basis.at[r * 64:r * 64 + 64]) for r in range(4)]
            + [(t1_hbm, t1), (t2_hbm, t2), (coords_hbm, coords)]
            + [(c0_hbm.at[r * 2:r * 2 + 2], c0.at[r * 2:r * 2 + 2]) for r in range(4)]
            + [(c1_hbm, c1), (c2_hbm, c2)]
        )
    ]
    for c in loads:
        c.start()
    for c in loads[:11]:
        c.wait()
    top = upward(coords, x, basis, t1, t2, pack)
    part[...] = jnp.where(lanes_low((32, 128)), top[:32], top[32:])
    pl.semaphore_wait(barrier, LANES + GROUPS - 1)

    def part_copy(d):
        peer = lax.rem(group + d, GROUPS)
        return (
            pltpu.make_async_remote_copy(
                part, parts.at[group], part_send.at[d], part_recv.at[group], (peer, lane), MESH
            ),
            pltpu.make_async_remote_copy(
                part, parts.at[peer], part_send.at[d], part_recv.at[peer], (peer, lane), MESH
            ),
        )

    def y2_copy(d):
        peer = lax.rem(lane + d, LANES)
        return (
            pltpu.make_async_remote_copy(
                y2_part, y2_parts.at[lane], y2_send.at[d], y2_recv.at[lane], (group, peer), MESH
            ),
            pltpu.make_async_remote_copy(
                y2_part, y2_parts.at[peer], y2_send.at[d], y2_recv.at[peer], (group, peer), MESH
            ),
        )

    def swap(src, dst, i, device):
        return pltpu.make_async_remote_copy(src, dst, swap_send.at[i], swap_recv.at[i], device, MESH)

    swaps = [
        swap(pack, p2, 0, beyond),
        swap(pack, p1, 1, partner),
        swap(x, x1, 2, partner),
        swap(x, x2_ref, 3, beyond),
    ]
    for d in range(1, GROUPS):
        part_copy(d)[0].start()
    for c in swaps:
        c.start()

    eye = identity()
    for leaf in range(LEAF):
        targets[leaf] = leaf_rows(pack, leaf)
        prepare(pack, x, leaf, leaf, eye, centres, feats, xs)
        acc[leaf] = jnp.zeros((64, PTS), f32)
    centres[2 * LEAF] = jnp.zeros((8, PTS), f32)
    feats[2 * LEAF] = feats[0]
    xs[2 * LEAF] = jnp.zeros((128, PTS), bf16)

    def leaves(i, _):
        at = [STEP * i + u for u in range(STEP) for s in range(SLOTS)]
        js = [list_ref[s, STEP * i + u] for u in range(STEP) for s in range(SLOTS)]
        pairs(at, [jnp.where(j == LEAF, 2 * LEAF, j) for j in js], targets, centres, feats, xs, acc)
        return 0

    lax.fori_loop(0, 1, leaves, 0)

    for c in loads[11:]:
        c.wait()
    for d in range(1, GROUPS):
        part_copy(d)[1].wait_recv()
    parts[group] = part[...]
    mine = top_coupled([parts[far2_ref[f, group]] for f in range(FAR2)], c2)
    y2_part[...] = mine
    y2_parts[lane] = mine
    for d in range(1, LANES):
        y2_copy(d)[0].start()

    lax.fori_loop(1, LEAF // STEP, leaves, 0)

    for c in swaps[:2]:
        c.wait()
    for b, p in enumerate((pack, p1, p2)):
        for t in range(LEAF // 2):
            place_tile(p[t], q_low, q_high, LEAF * b + 2 * t)
        for t in range(MID // 2):
            place_tile(p[LEAF // 2 + t], m_low, m_high, MID * b + 2 * t)
    for t in range(MID // 2):
        at = slice(t * 128, t * 128 + 128)
        y1_part[t] = coupled(
            [[source_of(far1_ref[f, 2 * t + i], place, MID) for f in range(FAR1)] for i in range(2)],
            [c1[f, :, at] for f in range(FAR1)], m_low, m_high,
        )

    def across(m, _):
        for u in range(2):
            t = 2 * m + u
            at = pl.ds(pl.multiple_of(t * 128, 128), 128)
            y0[t] = coupled(
                [[source_of(far0_ref[f, 2 * t + i], place, LEAF) for f in range(FAR0)] for i in range(2)],
                [c0[f, :, at] for f in range(FAR0)], q_low, q_high,
            )
        return 0

    lax.fori_loop(0, MID, across, 0)

    swaps[2].wait()
    for leaf in range(LEAF):
        prepare(p1, x1, leaf, LEAF + leaf, eye, centres, feats, xs)
    outs = [
        pltpu.make_async_copy(src, dst, out_sem.at[i])
        for i, (src, dst) in enumerate(
            [
                (pack, pack_out), (p2, p2_ref), (centres.at[0:48], centres_out),
                (feats.at[0:24], feats_out.at[0:24]), (feats.at[24:48], feats_out.at[24:48]),
                (xs.at[0:24], xs_out.at[0:24]), (xs.at[24:48], xs_out.at[24:48]),
                (acc, acc_out),
            ]
        )
    ]
    for c in outs[:-1]:
        c.start()

    for d in range(1, LANES):
        y2_copy(d)[1].wait_recv()
    y2 = y2_parts[0]
    for r in range(1, LANES):
        y2 = y2 + y2_parts[r]
    other = swap_halves(y2)
    low = lanes_low(y2.shape)
    y2 = jnp.concatenate([jnp.where(low, y2, other), jnp.where(low, other, y2)], axis=0)
    for t in range(MID // 2):
        w = t2[:, t * 128:t * 128 + 128]
        one, two = transposed(*halves(y2), jnp.concatenate([w, w], axis=0))
        y = y1_part[t] + jnp.where(lanes_low(one.shape), one, two)
        other = swap_halves(y)
        low = lanes_low(y.shape)
        y1[2 * t] = jnp.where(low, y, other)
        y1[2 * t + 1] = jnp.where(low, other, y)

    for m in range(MID):
        for u in range(2):
            t = 2 * m + u
            at = slice(t * 128, t * 128 + 128)
            w = t1[:, at]
            one, two = transposed(*halves(y1[m]), jnp.concatenate([w, w], axis=0))
            y = y0[t] + jnp.where(lanes_low(one.shape), one, two)
            one, two = transposed(*halves(y), basis[:, at])
            acc[2 * t] += one
            acc[2 * t + 1] += two
    outs[-1].start()
    for d in range(1, GROUPS):
        part_copy(d)[0].wait_send()
    for d in range(1, LANES):
        y2_copy(d)[0].wait_send()

    swaps[3].wait()
    for c in outs:
        c.wait()


def rest_kernel(
    list_ref, own_hbm, p2_hbm, x2_hbm, acc_hbm, centres_hbm, feats_hbm, xs_hbm, out_ref,
    own, p2, targets, centres, feats, xs, acc, x, sem, out_sem,
):
    moves = [
        pltpu.make_async_copy(src, dst, sem.at[i])
        for i, (src, dst) in enumerate(
            [(own_hbm, own), (p2_hbm, p2)]
            + [(x2_hbm.at[:, c * 1536:c * 1536 + 1536], x.at[:, c * 1536:c * 1536 + 1536]) for c in range(4)]
            + [
                (acc_hbm, acc.at[0:24]), (centres_hbm, centres.at[0:48]),
                (feats_hbm.at[0:24], feats.at[0:24]), (feats_hbm.at[24:48], feats.at[24:48]),
                (xs_hbm.at[0:24], xs.at[0:24]), (xs_hbm.at[24:48], xs.at[24:48]),
            ]
        )
    ]
    for c in moves:
        c.start()
    targets[LEAF] = jnp.zeros((8, PTS), f32)
    acc[LEAF] = jnp.zeros((64, PTS), f32)
    eye = identity()
    for c in moves[:6]:
        c.wait()
    for leaf in range(LEAF):
        targets[leaf] = leaf_rows(own, leaf)
        prepare(p2, x, leaf, 2 * LEAF + leaf, eye, centres, feats, xs)
    for c in moves[6:]:
        c.wait()

    @pl.loop(0, (list_ref[COUNT_ROW, 0] + (UNROLL - 1)) // UNROLL)
    def _(i):
        words = [list_ref[REST_ROW, i * UNROLL + u] for u in range(UNROLL)]
        pairs(
            [lax.shift_right_logical(w, 7) for w in words], [w & 127 for w in words], targets, centres, feats, xs, acc
        )

    outs = [
        pltpu.make_async_copy(acc.at[leaf], out_ref.at[:, leaf * PTS:leaf * PTS + PTS], out_sem.at[leaf])
        for leaf in range(LEAF)
    ]
    for c in outs:
        c.start()
    for c in outs:
        c.wait()


VM = pl.BlockSpec(memory_space=pltpu.VMEM)
SM = pl.BlockSpec(memory_space=pltpu.SMEM)
ANY = pl.BlockSpec(memory_space=pl.ANY)
DMA = pltpu.SemaphoreType.DMA


def params(mib, **more):
    return pltpu.CompilerParams(vmem_limit_bytes=mib << 20, **more)


def cost(size):
    return pl.CostEstimate(flops=size, bytes_accessed=1000, transcendentals=0)


def shape(*dims, dtype=f32):
    return jax.ShapeDtypeStruct(dims, dtype)


def local(
    coords, charges, basis, transfer1, transfer2, coupling0, coupling1, coupling2, near_list, near_count, far0_list,
    far1_list, far2_list,
):
    lists = pl.pallas_call(
        list_kernel, out_shape=shape(16, PTS, dtype=jnp.int32), in_specs=[VM, VM], out_specs=VM,
        compiler_params=params(56), cost_estimate=cost(1000), name="lists",
    )(near_list.T, near_count.reshape(1, LEAF))
    wide = LEAF * PTS
    acc, pack, p2, x2, centres, feats, xs = pl.pallas_call(
        main_kernel,
        out_shape=(
            shape(LEAF, 64, PTS), shape(18, 64, 128), shape(18, 64, 128), shape(64, wide), shape(2 * LEAF, 8, PTS),
            shape(2 * LEAF, PTS, 128, dtype=bf16), shape(2 * LEAF, 128, PTS, dtype=bf16),
        ),
        in_specs=[SM] * 4 + [ANY] * 8,
        out_specs=(ANY,) * 7,
        scratch_shapes=[
            pltpu.VMEM((3, wide), f32), pltpu.VMEM((64, wide), f32), pltpu.VMEM((64, wide), f32),
            pltpu.VMEM((PTS, LEAF * RANK), f32), pltpu.VMEM((RANK, LEAF * RANK), f32),
            pltpu.VMEM((RANK, MID * RANK), f32), pltpu.VMEM((FAR0, RANK, LEAF * RANK), f32),
            pltpu.VMEM((FAR1, RANK, MID * RANK), f32), pltpu.VMEM((FAR2, RANK, RANK), f32),
            pltpu.VMEM((18, 64, 128), f32), pltpu.VMEM((18, 64, 128), f32), pltpu.VMEM((18, 64, 128), f32),
            pltpu.VMEM((LEAF, 64, PTS), f32), pltpu.VMEM((LEAF, 8, PTS), f32),
            pltpu.VMEM((2 * LEAF + 1, 8, PTS), f32), pltpu.VMEM((2 * LEAF + 1, PTS, 128), bf16),
            pltpu.VMEM((2 * LEAF + 1, 128, PTS), bf16),
            pltpu.VMEM((32, 128), f32), pltpu.VMEM((GROUPS, 32, 128), f32), pltpu.VMEM((32, 128), f32),
            pltpu.VMEM((LANES, 32, 128), f32), pltpu.VMEM((MID, 64, 128), f32),
            pltpu.VMEM((MID // 2, 64, 128), f32), pltpu.VMEM((LEAF // 2, 64, 128), f32),
            pltpu.VMEM((3 * LEAF, 128, 128), bf16), pltpu.VMEM((3 * LEAF, 128, 128), bf16),
            pltpu.VMEM((3 * MID, 128, 128), bf16), pltpu.VMEM((3 * MID, 128, 128), bf16),
            DMA((17,)), DMA((GROUPS,)), DMA((GROUPS,)), DMA((LANES,)), DMA((LANES,)), DMA((4,)), DMA((4,)),
            DMA((8,)),
        ],
        compiler_params=params(56, collective_id=0, has_side_effects=True),
        cost_estimate=cost(1000),
        name="main",
    )(
        lists, far0_list.T, far1_list.T, far2_list.T, coords, charges, basis, transfer1, transfer2, coupling0,
        coupling1, coupling2,
    )
    return pl.pallas_call(
        rest_kernel,
        out_shape=shape(64, wide),
        in_specs=[SM] + [ANY] * 7,
        out_specs=ANY,
        scratch_shapes=[
            pltpu.VMEM((18, 64, 128), f32), pltpu.VMEM((18, 64, 128), f32), pltpu.VMEM((LEAF + 1, 8, PTS), f32),
            pltpu.VMEM((3 * LEAF, 8, PTS), f32), pltpu.VMEM((3 * LEAF, PTS, 128), bf16),
            pltpu.VMEM((3 * LEAF, 128, PTS), bf16), pltpu.VMEM((LEAF + 1, 64, PTS), f32), pltpu.VMEM((64, wide), f32),
            DMA((12,)), DMA((LEAF,)),
        ],
        compiler_params=params(56),
        cost_estimate=cost(1000),
        name="rest",
    )(lists, pack, p2, x2, acc, centres, feats, xs)


def solution(mesh):
    placed = (
        P(None, AXES),
        P(None, AXES),
        P(None, AXES),
        P(None, AXES),
        P(None, AXES),
        P(None, None, AXES),
        P(None, None, AXES),
        P(None, None, "grp"),
        P(AXES, None),
        P(AXES),
        P(AXES, None),
        P(AXES, None),
        P(),
    )
    return jax.shard_map(local, mesh=mesh, in_specs=placed, out_specs=P(None, AXES), check_vma=False)
```
